512 devices in a mesh: gz: 32 (over y, z_lo), gy: 4 (over z_hi, core), gx: 4 (over x).
Axes of the slice: x: 4, y: 4, z: 16 (z_hi: 2, z_lo: 8; z = z_hi * 8 + z_lo), core: 2. Of those that a mesh axis runs over, the one named last changes fastest.
Arguments:
- images: bfloat16 [32, 320, 2560], P('gz', 'gy', 'gx'), may hold values from -6 to 6
- partner: int32 [4, 4, 32], P('gy', 'gx'), may hold values from 0 to 31, each once within a row
- patch_mask: int32 [32, 4, 32], P('gz', 'gy', 'gx'), may hold values 0 or 1
- flows: bfloat16 [32, 4, 4, 8, 2], P('gz', 'gy', 'gx'), may hold values from -22 to 22
- dest_count: int32 [32, 4, 4, 8], P('gz', 'gy', 'gx'), may hold values from 1 to 2
- dest_owner: int32 [32, 4, 4, 8, 2], P('gz', 'gy', 'gx'), may hold values from 0 to 15, as said below
- dest_cell: int32 [32, 4, 4, 8, 2], P('gz', 'gy', 'gx'), may hold values from 0 to 7
Outputs:
- correlation: float32 [32, 4, 32, 160, 160], P('gz', 'gy', 'gx')
- warped: float32 [32, 320, 2560], P('gz', 'gy', 'gx')
The draws below stay inside these ranges and needn't reach their ends.
Inputs may be any that keep to these rules, and one draw needn't show every extreme that they name: `partner`: for each tile, a permutation of the 32 sections. `patch_mask`: 1 marks a valid patch. `dest_owner`: owner tiles are numbered tile row times 4 plus tile column, in the block's own section. Counting every entry, live or not, no owner is named more than 2 times by the entries of one tile; in each section one owner is named exactly 2 times by the first entries of every tile of that section. `dest_cell`: cells of the owner tile are numbered row-major over its 1 x 8 cells.
All inputs are finite; a program needn't handle non-finite values. No bound on the sum of `patch_mask` on one device may be relied on, other than what follows from the above.
Results may differ from the reference program's by a relative error of at most 0.0029.
Values may be sent and summed in bfloat16 or wider, within the bound.
A program may use at most 64 MiB of HBM per device.

```python
import jax
import jax.numpy as jnp
from jax import lax

PATCH_SIZE = 160
STRIDE = 80
HALO_WIDTH = 40
PATCH_ROWS = 1
PATCH_COLS = 8
MARGIN = 24
DEST_SLOTS = 2
BLOCKS = 8
PADDED = 128
CAPACITY = 2
TILE_HEIGHT = 80
TILE_WIDTH = 640
SECTIONS = 32
TILE_ROWS = 4
TILE_COLS = 4
OWNERS = 16
GRID_ROWS = 4
GRID_COLS = 32
IMAGE_ROWS = 320
IMAGE_COLS = 2560


def draw_dest_owner(key, part):
    sources = SECTIONS * OWNERS
    entries = BLOCKS * DEST_SLOTS
    spare = entries - CAPACITY
    hot_owner = jax.random.randint(jax.random.fold_in(key, 11), (SECTIONS,), 0, OWNERS)
    hot_owner = jnp.repeat(hot_owner, OWNERS)
    slot_keys = jax.random.split(jax.random.fold_in(key, 12), sources)
    block_keys = jax.random.split(jax.random.fold_in(key, 13), sources)
    shuffled = jax.vmap(lambda subkey: jax.random.permutation(subkey, (OWNERS - 1) * CAPACITY))(slot_keys)[:, :spare]
    ranked = jax.vmap(lambda subkey: jax.random.permutation(subkey, BLOCKS))(block_keys)
    others = shuffled // CAPACITY
    others = others + (others >= hot_owner[:, None]).astype(jnp.int32)
    position = jnp.arange(entries, dtype=jnp.int32)
    leading = position % DEST_SLOTS == 0
    block_of = jnp.broadcast_to((position // DEST_SLOTS)[None, :], (sources, entries))
    is_hot = leading[None, :] & (jnp.take_along_axis(ranked, block_of, axis=1) < CAPACITY)
    placing = jnp.cumsum(1 - is_hot.astype(jnp.int32), axis=1) - 1
    placing = jnp.clip(placing, 0, spare - 1)
    picked = jnp.take_along_axis(others, placing, axis=1)
    owners = jnp.where(is_hot, hot_owner[:, None], picked)
    return owners.reshape(SECTIONS, TILE_ROWS, TILE_COLS, BLOCKS, DEST_SLOTS).astype(jnp.int32)


def set_ends(drawn, stream_key, least, largest):
    place = [jax.random.randint(jax.random.fold_in(stream_key, axis), (), 0, length) for axis, length in enumerate(drawn.shape)]
    longest = drawn.shape.index(max(drawn.shape))
    neighbour = place[:longest] + [(place[longest] + 1) % drawn.shape[longest]] + place[longest + 1:]
    return drawn.at[tuple(place)].set(least).at[tuple(neighbour)].set(largest)


def block_levels(own_key, dims, cuts, smallest, largest):
    def one(dim, blocks):
        draws = jax.random.uniform(jax.random.fold_in(jax.random.fold_in(own_key, 6), dim), (blocks,), jnp.float32, smallest / len(cuts), largest / len(cuts))
        return jnp.repeat(jnp.exp(draws), dims[dim] // blocks).reshape((-1,) + (1,) * (len(dims) - dim - 1))

    gain = one(*cuts[0])
    for cut in cuts[1:]:
        gain = gain * one(*cut)
    return gain


def noise(key, shape, width, limit, cuts=(), held_as=jnp.bfloat16):
    factor_of = block_levels(key, shape, cuts, -0.22, 0.18) if cuts else 1.0
    values = jax.random.normal(key, shape, jnp.float32) * width * factor_of
    return jnp.minimum(jnp.maximum(values, -limit), limit).astype(held_as)


def setup_inputs(seed: int = 0) -> dict:
    arg_keys = jax.random.split(jax.random.key(seed), 8)
    images = noise(arg_keys[0], (SECTIONS, IMAGE_ROWS, IMAGE_COLS), 1.0, 6.0, ((0, 32), (1, 4), (2, 4)))
    partner = jax.vmap(lambda own: jax.random.permutation(own, SECTIONS))(jax.random.split(arg_keys[1], TILE_ROWS * TILE_COLS)).reshape((TILE_ROWS, TILE_COLS, SECTIONS)).astype(jnp.int32)
    patch_mask = set_ends((jax.random.randint(arg_keys[2], (SECTIONS, GRID_ROWS, GRID_COLS), 0, 4) < 3).astype(jnp.int32), jax.random.fold_in(arg_keys[2], 1), 0, 1)
    flows = jnp.clip(jax.random.uniform(arg_keys[3], (SECTIONS, TILE_ROWS, TILE_COLS, BLOCKS, 2), jnp.float32, -22.0, 22.0) * block_levels(arg_keys[3], (SECTIONS, TILE_ROWS, TILE_COLS, BLOCKS, 2), ((0, 32), (1, 4), (2, 4)), -0.4, 0.0), -22.0, 22.0).astype(jnp.bfloat16)
    dest_count = set_ends(jax.random.randint(arg_keys[4], (SECTIONS, TILE_ROWS, TILE_COLS, BLOCKS), 1, DEST_SLOTS + 1), jax.random.fold_in(arg_keys[4], 1), 1, DEST_SLOTS).astype(jnp.int32)
    dest_owner = draw_dest_owner(jax.random.fold_in(arg_keys[7], 71), 0)
    dest_cell = set_ends(jax.random.randint(arg_keys[6], (SECTIONS, TILE_ROWS, TILE_COLS, BLOCKS, DEST_SLOTS), 0, BLOCKS), jax.random.fold_in(arg_keys[6], 1), 0, BLOCKS - 1).astype(jnp.int32)
    return dict(images=images, partner=partner, patch_mask=patch_mask, flows=flows, dest_count=dest_count, dest_owner=dest_owner, dest_cell=dest_cell)


epsilon = 1e-05

def patch_grid(padded):
    rows = padded.shape[0] // STRIDE
    columns = padded.shape[1] // STRIDE
    cells = padded.reshape(rows, STRIDE, columns, STRIDE).transpose(0, 2, 1, 3)
    upper = jnp.concatenate([cells[:-1, :-1], cells[:-1, 1:]], axis=-1)
    lower = jnp.concatenate([cells[1:, :-1], cells[1:, 1:]], axis=-1)
    return jnp.concatenate([upper, lower], axis=-2)

def standardize(patches):
    centred = patches - lax.optimization_barrier(jnp.mean(patches, axis=(-2, -1), keepdims=True))
    spread = lax.optimization_barrier(jnp.mean(centred * centred, axis=(-2, -1), keepdims=True))
    return centred / jnp.sqrt(spread + epsilon)

def interp_weights(shift):
    shift = shift.astype(jnp.float32)
    target = jnp.arange(PADDED, dtype=jnp.int32).astype(shift.dtype)
    source = jnp.arange(STRIDE, dtype=jnp.int32).astype(shift.dtype)
    offset = target[:, None] - MARGIN - shift[..., None, None] - source[None, :]
    return jnp.maximum(1.0 - jnp.abs(offset), 0.0)

def warp_blocks(blocks, shifts):
    row_weight = interp_weights(shifts[..., 0])
    column_weight = interp_weights(shifts[..., 1])
    middle = jnp.einsum('...ps,...st->...pt', row_weight, blocks.astype(row_weight.dtype), precision=lax.Precision.HIGHEST)
    result = jnp.einsum('...pt,...qt->...pq', middle, column_weight, precision=lax.Precision.HIGHEST)
    return result.astype(jnp.bfloat16)

def matched_image(index, images, partner):
    tiles = images.reshape(SECTIONS, TILE_ROWS, TILE_HEIGHT, TILE_COLS, TILE_WIDTH)
    chosen = partner[:, :, index].astype(jnp.int32)
    row_ids = jnp.arange(TILE_ROWS, dtype=jnp.int32)[:, None]
    column_ids = jnp.arange(TILE_COLS, dtype=jnp.int32)[None, :]
    picked = tiles[chosen, row_ids, :, column_ids, :]
    return picked.transpose(0, 2, 1, 3).reshape(IMAGE_ROWS, IMAGE_COLS)

def section_correlation(index, images, partner, patch_mask):
    own_image = images[index].astype(jnp.float32)
    other_image = matched_image(index, images, partner).astype(jnp.float32)
    own_norm = standardize(patch_grid(jnp.pad(own_image, HALO_WIDTH)))
    other_norm = standardize(patch_grid(jnp.pad(other_image, HALO_WIDTH)))
    spectrum = jnp.conj(jnp.fft.fft2(own_norm)) * jnp.fft.fft2(other_norm)
    values = jnp.real(jnp.fft.ifft2(spectrum)) / PATCH_SIZE
    weight = patch_mask[index].astype(values.dtype)
    return (values * weight[:, :, None, None]).astype(jnp.float32)

def section_warp(index, images, flows, dest_count, dest_owner, dest_cell):
    image = images[index]
    tiles = image.reshape(TILE_ROWS, PATCH_ROWS, STRIDE, TILE_COLS, PATCH_COLS, STRIDE)
    blocks = tiles.transpose(0, 3, 1, 4, 2, 5).reshape(OWNERS, BLOCKS, STRIDE, STRIDE)
    partial_value = warp_blocks(blocks, flows[index].reshape(OWNERS, BLOCKS, 2))
    live = jnp.arange(DEST_SLOTS, dtype=jnp.int32)[None, None, :] < dest_count[index].reshape(OWNERS, BLOCKS, 1)
    target = dest_owner[index].reshape(OWNERS, BLOCKS, DEST_SLOTS) * BLOCKS + dest_cell[index].reshape(OWNERS, BLOCKS, DEST_SLOTS)
    target = jnp.where(live, target, OWNERS * BLOCKS).reshape(-1)
    source = jnp.broadcast_to(jnp.arange(OWNERS * BLOCKS, dtype=jnp.int32).reshape(OWNERS, BLOCKS, 1), (OWNERS, BLOCKS, DEST_SLOTS)).reshape(-1)
    values = partial_value.reshape(OWNERS * BLOCKS, PADDED, PADDED).astype(jnp.float32)[source]
    sums = jax.ops.segment_sum(values, target, num_segments=OWNERS * BLOCKS + 1)[:-1]
    sums = sums.reshape(OWNERS, PATCH_ROWS, PATCH_COLS, PADDED, PADDED)
    canvas = jnp.zeros((OWNERS, TILE_HEIGHT + 2 * MARGIN, TILE_WIDTH + 2 * MARGIN), sums.dtype)
    for row_index in range(PATCH_ROWS):
        for column_index in range(PATCH_COLS):
            canvas = canvas.at[:, STRIDE * row_index:STRIDE * row_index + PADDED, STRIDE * column_index:STRIDE * column_index + PADDED].add(sums[:, row_index, column_index])
    inner = canvas[:, MARGIN:MARGIN + TILE_HEIGHT, MARGIN:MARGIN + TILE_WIDTH]
    return inner.reshape(TILE_ROWS, TILE_COLS, TILE_HEIGHT, TILE_WIDTH).transpose(0, 2, 1, 3).reshape(IMAGE_ROWS, IMAGE_COLS)

def reference(images, partner, patch_mask, flows, dest_count, dest_owner, dest_cell):
    order = jnp.arange(SECTIONS, dtype=jnp.int32)
    correlation = lax.map(lambda index: section_correlation(index, images, partner, patch_mask), order)
    warped = lax.map(lambda index: section_warp(index, images, flows, dest_count, dest_owner, dest_cell), order)
    return (correlation, warped)
```

```python
import functools

import jax
import jax.numpy as jnp
import ml_dtypes
import numpy as np
from jax import lax
from jax.experimental import pallas as pl
from jax.experimental.pallas import tpu as pltpu
from jax.sharding import PartitionSpec as P

PATCH_SIZE = 160
STRIDE = 80
PATCH_COLS = 8
MARGIN = 24
DEST_SLOTS = 2
BLOCKS = 8
PADDED = 128
SECTIONS = 32
HEIGHT = 80
WIDTH = 640
CHUNKS = 25
LANES = 128
HALO_ROWS = 48
STRIP_ROWS = HEIGHT + 2 * HALO_ROWS
STRIP_COLS = WIDTH + 2 * LANES
HALVES = 9
WAVES = 88
FIXED = 24

epsilon = 1e-05
f32 = jnp.float32
bf16 = jnp.bfloat16
MESH = pl.DeviceIdType.MESH


def halves(table):
    high = table.astype(ml_dtypes.bfloat16)
    low = (table - high.astype(np.float64)).astype(ml_dtypes.bfloat16)
    return high, low


def make_tables():
    wave = np.arange(81)
    place = np.arange(PATCH_SIZE)
    angle = 2.0 * np.pi * (np.outer(wave, place) % PATCH_SIZE) / PATCH_SIZE
    cosine, sine = np.cos(angle), np.sin(angle)
    sine[0] = 0.0
    sine[80] = 0.0
    rows = np.zeros((2 * WAVES, PATCH_SIZE))
    rows[:81] = cosine
    rows[WAVES : WAVES + 81] = sine
    rows_high, rows_low = halves(rows)
    rows_both = np.concatenate([rows_high, rows_low], axis=0)
    row_sums = (rows_high.astype(np.float64) + rows_low.astype(np.float64)).sum(axis=1)
    row_sums = np.broadcast_to(row_sums[:, None], (2 * WAVES, LANES)).astype(np.float32)
    columns = np.zeros((LANES, 2 * LANES))
    columns[:STRIDE, :81] = cosine[:, :STRIDE].T
    columns[:STRIDE, LANES : LANES + 81] = sine[:, :STRIDE].T
    columns_high, columns_low = halves(columns)
    columns_twice = np.concatenate([columns_high, columns_high], axis=0)
    weight = np.ones(81)
    weight[0] = weight[80] = 0.5
    back_columns = np.zeros((2 * LANES, PATCH_SIZE))
    back_columns[:81] = weight[:, None] * cosine
    back_columns[LANES : LANES + 81] = weight[:, None] * sine
    back_columns = halves(back_columns)
    weight = np.full(81, 2.0)
    weight[0] = weight[80] = 1.0
    back_rows = np.zeros((PATCH_SIZE, 2 * WAVES))
    back_rows[:, :81] = (weight[:, None] * cosine).T
    back_rows[:, WAVES : WAVES + 81] = -(weight[:, None] * sine).T
    back_rows = halves(back_rows)
    return (rows_both, row_sums, columns_twice, columns_low, *back_columns, *back_rows)


def table_kernel(owner_ref, cell_ref, count_ref, flow_ref, table_ref, filled_ref):
    for index in range(32):
        table_ref[0, 4 * index] = 0
        table_ref[0, 4 * index + 1] = -1
        table_ref[0, 4 * index + 2] = 0
        table_ref[0, 4 * index + 3] = 0
    for index in range(16):
        filled_ref[index] = 0
    for block in range(BLOCKS):
        count = count_ref[block]
        for entry in range(DEST_SLOTS):

            @pl.when(entry < count)
            def _():
                owner = owner_ref[2 * block + entry]
                rank = filled_ref[owner]
                filled_ref[owner] = rank + 1
                base = 8 * owner + 4 * rank
                table_ref[0, base] = block
                table_ref[0, base + 1] = cell_ref[2 * block + entry]
                table_ref[0, base + 2] = flow_ref[2 * block]
                table_ref[0, base + 3] = flow_ref[2 * block + 1]


def chunk_of(index):
    line, place = index // 8, index % 8
    holds = ((place >= 1) & (place <= 6)) | (index == 0)
    return holds, jnp.where(index == 0, CHUNKS - 1, line * 6 + place - 1)


def holder_of(chunk):
    return jnp.where(chunk == CHUNKS - 1, 0, (chunk // 6) * 8 + chunk % 6 + 1)


def chunk_at(ref, chunk, row, column):
    rows = pl.ds(pl.multiple_of(row + 16 * (chunk // 5), 16), 16)
    columns = pl.ds(pl.multiple_of(column + LANES * (chunk % 5), LANES), LANES)
    return ref.at[rows, columns]


def exchange_kernel(
    tile_ref,
    partner_ref,
    table_ref,
    table_smem,
    own_ref,
    other_ref,
    slots_ref,
    info_ref,
    held,
    sorted_,
    mirror,
    blocks,
    outgoing,
    tables,
    mirror_smem,
    send_sem,
    recv_sem,
    far_sem,
    slot_sem,
    local_sem,
):
    gz, gy, gx = lax.axis_index("gz"), lax.axis_index("gy"), lax.axis_index("gx")
    half, core = gy // 2, gy % 2
    place = core * 4 + gx
    far_gy = 3 - gy
    near_gy = gy + 1 - 2 * core

    barrier = pltpu.get_barrier_semaphore()

    def greet(step, carry):
        pl.semaphore_signal(
            barrier, inc=1, device_id={"gz": lax.rem(gz + step, SECTIONS)}, device_id_type=MESH
        )
        return carry

    lax.fori_loop(1, SECTIONS, greet, 0)
    for step in range(1, 8):
        other_place = lax.rem(place + step, 8)
        pl.semaphore_signal(
            barrier,
            inc=1,
            device_id={"gy": 2 * half + other_place // 4, "gx": other_place % 4},
            device_id_type=MESH,
        )
    pl.semaphore_signal(barrier, inc=1, device_id={"gy": far_gy}, device_id_type=MESH)

    tables[0] = table_ref[...]
    own_ref[pl.ds(HALO_ROWS, HEIGHT), pl.ds(LANES, WIDTH)] = tile_ref[...]
    top, bottom = pl.ds(0, HALO_ROWS), pl.ds(HALO_ROWS + HEIGHT, HALO_ROWS)
    left, right = pl.ds(0, LANES), pl.ds(LANES + WIDTH, LANES)
    middle = pl.ds(LANES, WIDTH)
    for ref in (own_ref, other_ref):

        @pl.when(gy == 0)
        def _():
            ref[top, middle] = jnp.zeros((HALO_ROWS, WIDTH), bf16)

        @pl.when(gy == 3)
        def _():
            ref[bottom, middle] = jnp.zeros((HALO_ROWS, WIDTH), bf16)

        @pl.when(gx == 0)
        def _():
            ref[:, left] = jnp.zeros((STRIP_ROWS, LANES), bf16)

        @pl.when(gx == 3)
        def _():
            ref[:, right] = jnp.zeros((STRIP_ROWS, LANES), bf16)

    holds, mine = chunk_of(gz)
    pl.semaphore_wait(barrier, SECTIONS - 1 + 8)

    def scatter(step, carry):
        chunk = lax.rem(mine + step, CHUNKS)
        holder = holder_of(chunk)

        @pl.when(holder != gz)
        def _():
            pltpu.make_async_remote_copy(
                src_ref=chunk_at(tile_ref, chunk, 0, 0),
                dst_ref=held.at[gz],
                send_sem=send_sem.at[0],
                recv_sem=recv_sem.at[0],
                device_id={"gz": holder},
                device_id_type=MESH,
            ).start()

        return carry

    lax.fori_loop(0, CHUNKS, scatter, 0)

    def copy(src, dst, slot, device):
        return pltpu.make_async_remote_copy(
            src_ref=src,
            dst_ref=dst,
            send_sem=far_sem.at[0, slot],
            recv_sem=far_sem.at[1, slot],
            device_id=device,
            device_id_type=MESH,
        )

    near = {"gy": near_gy}

    own_down = copy(
        tile_ref.at[pl.ds(HEIGHT - HALO_ROWS, HALO_ROWS), :], own_ref.at[top, middle], 0, near
    )
    own_up = copy(tile_ref.at[pl.ds(0, HALO_ROWS), :], own_ref.at[bottom, middle], 0, near)

    @pl.when(core == 0)
    def _():
        own_down.start()

    @pl.when(core == 1)
    def _():
        own_up.start()

    to_far = copy(tile_ref, mirror, 1, {"gy": far_gy})
    to_far.start()
    table_far = copy(tables.at[0], tables.at[1], 2, {"gy": far_gy})
    table_far.start()

    lane = lax.broadcasted_iota(jnp.int32, (HEIGHT, LANES), 1)

    def cut_blocks(ref, base):
        for block in range(BLOCKS):
            start = STRIDE * block
            first = start // LANES * LANES
            shift = start - first
            width = LANES if shift + STRIDE <= LANES else 2 * LANES
            window = ref[:, first : first + width].astype(f32)
            if shift:
                window = pltpu.roll(window, width - shift, 1)[:, :LANES]
            blocks[base + block] = jnp.where(lane < STRIDE, window, 0.0).astype(bf16)

    cut_blocks(tile_ref, 0)

    @pl.when(holds)
    def _():
        held[gz] = chunk_at(tile_ref, mine, 0, 0)[...]
        pltpu.make_async_copy(
            held.at[pl.ds(0, SECTIONS - 1)], held.at[pl.ds(0, SECTIONS - 1)], recv_sem.at[0]
        ).wait()

        def deliver(step, carry):
            section = lax.rem(gz + step, SECTIONS)
            sorted_[section] = held[partner_ref[section]]
            pltpu.make_async_remote_copy(
                src_ref=sorted_.at[section],
                dst_ref=chunk_at(other_ref, mine, HALO_ROWS, LANES),
                send_sem=send_sem.at[1],
                recv_sem=recv_sem.at[1],
                device_id={"gz": section},
                device_id_type=MESH,
            ).start()
            return carry

        lax.fori_loop(1, SECTIONS, deliver, 0)
        chunk_at(other_ref, mine, HALO_ROWS, LANES)[...] = held[partner_ref[gz]]

    def side_copies(ref, slot):
        to_right = copy(
            ref.at[:, pl.ds(WIDTH, LANES)], ref.at[:, left], slot, {"gx": jnp.minimum(gx + 1, 3)}
        )
        to_left = copy(
            ref.at[:, pl.ds(LANES, LANES)], ref.at[:, right], slot + 1, {"gx": jnp.maximum(gx - 1, 0)}
        )
        return to_right, to_left

    def start_sides(copies):
        @pl.when(gx < 3)
        def _():
            copies[0].start()

        @pl.when(gx > 0)
        def _():
            copies[1].start()

    def receive_sides(copies):
        @pl.when(gx > 0)
        def _():
            copies[0].wait_recv()

        @pl.when(gx < 3)
        def _():
            copies[1].wait_recv()

    def sent_sides(copies):
        @pl.when(gx < 3)
        def _():
            copies[0].wait_send()

        @pl.when(gx > 0)
        def _():
            copies[1].wait_send()

    @pl.when(core == 1)
    def _():
        own_down.wait_recv()

    @pl.when(core == 0)
    def _():
        own_up.wait_recv()

    to_far.wait_recv()

    @pl.when(gy == 1)
    def _():
        own_ref[bottom, middle] = mirror[pl.ds(0, HALO_ROWS), :]

    @pl.when(gy == 2)
    def _():
        own_ref[top, middle] = mirror[pl.ds(HEIGHT - HALO_ROWS, HALO_ROWS), :]

    own_sides = side_copies(own_ref, 3)
    start_sides(own_sides)

    table_far.wait_recv()
    fetch = pltpu.make_async_copy(tables.at[1], mirror_smem, local_sem)
    fetch.start()
    cut_blocks(mirror, BLOCKS)
    fetch.wait()

    def fill(target, index):
        owner = 8 * half + target
        for kind, table in ((0, table_smem), (1, mirror_smem)):
            for rank in range(2):
                block = table[0, 8 * owner + 4 * rank]
                index[2 * kind + rank] = blocks[BLOCKS * kind + block]

    def send_slots(step, carry):
        target = lax.rem(place + step, 8)
        fill(target, outgoing.at[target])
        device = {"gy": 2 * half + target // 4, "gx": target % 4}
        for src, dst, kind in (
            (outgoing.at[target], slots_ref.at[place], 0),
            (tables, info_ref.at[place], 1),
        ):
            pltpu.make_async_remote_copy(
                src_ref=src,
                dst_ref=dst,
                send_sem=slot_sem.at[0, kind],
                recv_sem=slot_sem.at[1, kind],
                device_id=device,
                device_id_type=MESH,
            ).start()
        return carry

    lax.fori_loop(1, 8, send_slots, 0)
    fill(place, slots_ref.at[place])
    info_ref[place] = tables[...]

    chunks = held.at[pl.ds(0, CHUNKS)]
    fewer = held.at[pl.ds(0, CHUNKS - 1)]

    @pl.when(holds)
    def _():
        pltpu.make_async_copy(fewer, fewer, recv_sem.at[1]).wait()

    @pl.when(jnp.logical_not(holds))
    def _():
        pltpu.make_async_copy(chunks, chunks, recv_sem.at[1]).wait()

    rows_up = pl.ds(HALO_ROWS, HALO_ROWS)
    rows_down = pl.ds(HEIGHT, HALO_ROWS)
    other_down = copy(
        other_ref.at[rows_down, middle], other_ref.at[top, middle], 5, {"gy": jnp.minimum(gy + 1, 3)}
    )
    other_up = copy(
        other_ref.at[rows_up, middle], other_ref.at[bottom, middle], 6, {"gy": jnp.maximum(gy - 1, 0)}
    )

    @pl.when(gy < 3)
    def _():
        other_down.start()

    @pl.when(gy > 0)
    def _():
        other_up.start()

    @pl.when(gy > 0)
    def _():
        other_down.wait_recv()

    @pl.when(gy < 3)
    def _():
        other_up.wait_recv()

    other_sides = side_copies(other_ref, 7)
    start_sides(other_sides)

    receive_sides(own_sides)
    seven = slots_ref.at[pl.ds(0, 7)]
    pltpu.make_async_copy(seven, seven, slot_sem.at[1, 0]).wait()
    seven_info = info_ref.at[pl.ds(0, 7)]
    pltpu.make_async_copy(seven_info, seven_info, slot_sem.at[1, 1]).wait()
    receive_sides(other_sides)

    pltpu.make_async_copy(seven, seven, slot_sem.at[0, 0]).wait()
    pltpu.make_async_copy(seven_info, seven_info, slot_sem.at[0, 1]).wait()

    @pl.when(holds)
    def _():
        pltpu.make_async_copy(fewer, fewer, send_sem.at[0]).wait()
        all_but_one = held.at[pl.ds(0, SECTIONS - 1)]
        pltpu.make_async_copy(all_but_one, all_but_one, send_sem.at[1]).wait()

    @pl.when(jnp.logical_not(holds))
    def _():
        pltpu.make_async_copy(chunks, chunks, send_sem.at[0]).wait()

    @pl.when(core == 0)
    def _():
        own_down.wait_send()

    @pl.when(core == 1)
    def _():
        own_up.wait_send()

    to_far.wait_send()
    table_far.wait_send()

    @pl.when(gy < 3)
    def _():
        other_down.wait_send()

    @pl.when(gy > 0)
    def _():
        other_up.wait_send()

    sent_sides(own_sides)
    sent_sides(other_sides)


def split(value):
    high = value.astype(bf16)
    return high, (value - high.astype(f32)).astype(bf16)


def dot(left, right):
    return jnp.dot(left, right, preferred_element_type=f32)


def compute_kernel(
    own_ref,
    other_ref,
    slots_ref,
    info_ref,
    mask_ref,
    place_ref,
    rows_both,
    row_sums,
    columns_twice,
    columns_low,
    back_columns_high,
    back_columns_low,
    back_rows_high,
    back_rows_low,
    correlation_ref,
    warped_ref,
    strip,
    spectra,
    parts,
    cells,
    shifted,
    canvas,
):
    lane = lax.broadcasted_iota(jnp.int32, (PATCH_SIZE, LANES), 1)
    means, squares = [], []
    for index, ref in enumerate((own_ref, other_ref)):
        for block in range(HALVES):
            start = LANES - 40 + STRIDE * block
            first = start // LANES * LANES
            shift = start - first
            width = LANES if shift + STRIDE <= LANES else 2 * LANES
            window = ref[8 : 8 + PATCH_SIZE, first : first + width].astype(f32)
            window = pltpu.roll(window, width - shift, 1)[:, :LANES]
            window = jnp.where(lane < STRIDE, window, 0.0)
            mean = jnp.sum(window, keepdims=True) * (1.0 / (PATCH_SIZE * STRIDE))
            centred = jnp.where(lane < STRIDE, window - mean, 0.0)
            means.append(mean)
            squares.append(jnp.sum(centred * centred, keepdims=True))
            strip[:, pl.ds((index * HALVES + block) * LANES, LANES)] = window.astype(bf16)

    levels = [sum(means[:HALVES]) * (1.0 / HALVES), sum(means[HALVES:]) * (1.0 / HALVES)]
    for block in range(2 * HALVES):
        both = dot(rows_both[...], strip[:, pl.ds(block * LANES, LANES)])
        value = both[: 2 * WAVES] + both[2 * WAVES :] - levels[block // HALVES] * row_sums[...]
        high, low = split(value)
        spectra[block, :, :LANES] = high
        spectra[block, :, LANES:] = low
    for block in range(2 * HALVES):
        parts[block] = dot(spectra[block], columns_twice[...]) + dot(
            spectra[block, :, :LANES], columns_low[...]
        )

    row = lax.broadcasted_iota(jnp.int32, (WAVES, LANES), 0)
    column = lax.broadcasted_iota(jnp.int32, (WAVES, LANES), 1)
    constant = (row == 0) & (column == 0)
    odd = column % 2 == 1
    count = PATCH_SIZE * STRIDE

    def spectrum(first):
        def one(rows, lanes):
            later = parts[first + 1, rows, lanes]
            return parts[first, rows, lanes] + jnp.where(odd, -later, later)

        upper, lower = pl.ds(0, WAVES), pl.ds(WAVES, WAVES)
        low, high = pl.ds(0, LANES), pl.ds(LANES, LANES)
        a = jnp.where(constant, 0.0, one(upper, low))
        return a, one(lower, high), one(lower, low), one(upper, high)

    for patch in range(PATCH_COLS):
        scale = mask_ref[0, patch].astype(f32) * (1.0 / PATCH_SIZE**3)
        for base in (0, HALVES):
            first, second = base + patch, base + patch + 1
            gap = means[first] - means[second]
            spread = (squares[first] + squares[second] + gap * gap * (count / 2)) * (0.5 / count)
            scale = scale / jnp.sqrt(spread + epsilon)
        a, b, c, d = spectrum(patch)
        e, f, g, h = spectrum(HALVES + patch)
        scale = 2.0 * scale
        even_real = (a * e + b * f + c * g + d * h) * scale
        odd_real = (c * h + d * g - a * f - b * e) * scale
        even_imag = (c * e - d * f - a * g + b * h) * scale
        odd_imag = (d * e - c * f - a * h + b * g) * scale
        joined = jnp.concatenate(
            [
                jnp.concatenate([even_real, -odd_imag], axis=1),
                jnp.concatenate([even_imag, odd_real], axis=1),
            ],
            axis=0,
        )
        high, low = split(joined)
        half = (
            dot(high, back_columns_high[...])
            + dot(low, back_columns_high[...])
            + dot(high, back_columns_low[...])
        )
        high, low = split(half)
        correlation_ref[patch] = (
            dot(back_rows_high[...], high)
            + dot(back_rows_high[...], low)
            + dot(back_rows_low[...], high)
        )

    cells[...] = jnp.zeros_like(cells)
    shifted[...] = jnp.zeros_like(shifted)
    mine = place_ref[0] * 8

    def entry(index, carry):
        source, kind, rank = index // 4, index % 4 // 2, index % 2
        base = mine + 4 * rank
        cell = info_ref[source, kind, 0, base + 1]

        @pl.when(cell >= 0)
        def _():
            down, across = info_ref[source, kind, 0, base + 2], info_ref[source, kind, 0, base + 3]
            whole_down, whole_across = down >> FIXED, across >> FIXED
            unit = 1.0 / 2**FIXED
            part_down = (down & (2**FIXED - 1)).astype(f32) * unit
            part_across = (across & (2**FIXED - 1)).astype(f32) * unit
            block = slots_ref[source, 2 * kind + rank].astype(f32)
            here = pltpu.roll(block, whole_across + MARGIN, 1)
            after = pltpu.roll(block, whole_across + MARGIN + 1, 1)
            shifted[pl.ds(MARGIN, HEIGHT), :] = here * (1.0 - part_across) + after * part_across
            here = shifted[pl.ds(MARGIN - whole_down, HEIGHT), :]
            after = shifted[pl.ds(MARGIN - 1 - whole_down, HEIGHT), :]
            value = here * (1.0 - part_down) + after * part_down
            cells[cell] = cells[cell] + value.astype(bf16).astype(f32)

        return carry

    lax.fori_loop(0, 32, entry, 0)
    canvas[...] = jnp.zeros_like(canvas)
    for cell in range(BLOCKS):
        start = LANES - MARGIN + STRIDE * cell
        first = start // LANES * LANES
        shift = start - first
        wide = jnp.concatenate([cells[cell], jnp.zeros((HEIGHT, LANES), f32)], axis=1)
        if shift:
            wide = pltpu.roll(wide, shift, 1)
        canvas[:, first : first + 2 * LANES] = canvas[:, first : first + 2 * LANES] + wide
    warped_ref[...] = canvas[:, LANES : LANES + WIDTH]


VMEM = pl.BlockSpec(memory_space=pltpu.VMEM)
SMEM = pl.BlockSpec(memory_space=pltpu.SMEM)


def body(tables, images, partner, patch_mask, flows, dest_count, dest_owner, dest_cell):
    tile = images[0]
    fixed = jnp.round(flows.astype(f32) * float(2**FIXED)).astype(jnp.int32).reshape(16)
    table = pl.pallas_call(
        table_kernel,
        out_shape=jax.ShapeDtypeStruct((1, 128), jnp.int32),
        in_specs=[SMEM] * 4,
        out_specs=SMEM,
        scratch_shapes=[pltpu.SMEM((16,), jnp.int32)],
    )(dest_owner.reshape(16), dest_cell.reshape(16), dest_count.reshape(8), fixed)
    own, other, slots, info = pl.pallas_call(
        exchange_kernel,
        out_shape=[
            jax.ShapeDtypeStruct((STRIP_ROWS, STRIP_COLS), bf16),
            jax.ShapeDtypeStruct((STRIP_ROWS, STRIP_COLS), bf16),
            jax.ShapeDtypeStruct((8, 4, HEIGHT, LANES), bf16),
            jax.ShapeDtypeStruct((8, 2, 1, 128), jnp.int32),
        ],
        in_specs=[VMEM, SMEM, VMEM, SMEM],
        out_specs=[VMEM] * 4,
        scratch_shapes=[
            pltpu.VMEM((SECTIONS, 16, LANES), bf16),
            pltpu.VMEM((SECTIONS, 16, LANES), bf16),
            pltpu.VMEM((HEIGHT, WIDTH), bf16),
            pltpu.VMEM((2 * BLOCKS, HEIGHT, LANES), bf16),
            pltpu.VMEM((8, 4, HEIGHT, LANES), bf16),
            pltpu.VMEM((2, 1, 128), jnp.int32),
            pltpu.SMEM((1, 128), jnp.int32),
            pltpu.SemaphoreType.DMA((2,)),
            pltpu.SemaphoreType.DMA((2,)),
            pltpu.SemaphoreType.DMA((2, 9)),
            pltpu.SemaphoreType.DMA((2, 2)),
            pltpu.SemaphoreType.DMA,
        ],
        compiler_params=pltpu.CompilerParams(
            collective_id=0, has_side_effects=True, vmem_limit_bytes=24 * 2**20
        ),
    )(tile, partner.reshape(SECTIONS), table, table)
    place = (lax.axis_index("gy") * 4 + lax.axis_index("gx")).astype(jnp.int32).reshape(1)
    correlation, warped = pl.pallas_call(
        compute_kernel,
        out_shape=[
            jax.ShapeDtypeStruct((PATCH_COLS, PATCH_SIZE, PATCH_SIZE), f32),
            jax.ShapeDtypeStruct((HEIGHT, WIDTH), f32),
        ],
        in_specs=[VMEM, VMEM, VMEM, SMEM, SMEM, SMEM] + [VMEM] * 8,
        out_specs=[VMEM] * 2,
        scratch_shapes=[
            pltpu.VMEM((PATCH_SIZE, 2 * HALVES * LANES), bf16),
            pltpu.VMEM((2 * HALVES, 2 * WAVES, 2 * LANES), bf16),
            pltpu.VMEM((2 * HALVES, 2 * WAVES, 2 * LANES), f32),
            pltpu.VMEM((BLOCKS, HEIGHT, LANES), f32),
            pltpu.VMEM((128, LANES), f32),
            pltpu.VMEM((HEIGHT, STRIP_COLS), f32),
        ],
        compiler_params=pltpu.CompilerParams(vmem_limit_bytes=40 * 2**20),
    )(own, other, slots, info, patch_mask[0], place, *tables)
    return correlation[None, None], warped[None]


def solution(mesh):
    placed = (
        P("gz", "gy", "gx"),
        P("gy", "gx", None),
        P("gz", "gy", "gx"),
        P("gz", "gy", "gx", None, None),
        P("gz", "gy", "gx", None),
        P("gz", "gy", "gx", None, None),
        P("gz", "gy", "gx", None, None),
    )
    tables = tuple(jnp.asarray(table) for table in make_tables())
    return jax.shard_map(
        functools.partial(body, tables),
        mesh=mesh,
        in_specs=placed,
        out_specs=(P("gz", "gy", "gx", None, None), P("gz", "gy", "gx")),
        check_vma=False,
    )
```

```python
import functools

import jax
import jax.numpy as jnp
import ml_dtypes
import numpy as np
from jax import lax
from jax.experimental import pallas as pl
from jax.experimental.pallas import tpu as pltpu
from jax.sharding import PartitionSpec as P

PATCH_SIZE = 160
STRIDE = 80
PATCH_COLS = 8
MARGIN = 24
DEST_SLOTS = 2
BLOCKS = 8
OWNERS = 16
PADDED = 128
SECTIONS = 32
HEIGHT = 80
WIDTH = 640
CHUNKS = 25
LANES = 128
HALO_ROWS = 48
STRIP_ROWS = HEIGHT + 2 * HALO_ROWS
STRIP_COLS = WIDTH + 2 * LANES
HALVES = 9
WAVES = 88
VMEM_BYTES = 60 * 2**20
FIXED = 24

epsilon = 1e-05
f32 = jnp.float32
bf16 = jnp.bfloat16
MESH = pl.DeviceIdType.MESH


def halves(table):
    high = table.astype(ml_dtypes.bfloat16)
    low = (table - high.astype(np.float64)).astype(ml_dtypes.bfloat16)
    return high, low


def make_tables():
    wave = np.arange(81)
    place = np.arange(PATCH_SIZE)
    angle = 2.0 * np.pi * (np.outer(wave, place) % PATCH_SIZE) / PATCH_SIZE
    cosine, sine = np.cos(angle), np.sin(angle)
    sine[0] = 0.0
    sine[80] = 0.0
    rows = np.zeros((2 * WAVES, PATCH_SIZE))
    rows[:81] = cosine
    rows[WAVES : WAVES + 81] = sine
    rows_high, rows_low = halves(rows)
    rows_both = np.concatenate([rows_high, rows_low], axis=0)
    row_sums = (rows_high.astype(np.float64) + rows_low.astype(np.float64)).sum(axis=1)
    row_sums = np.broadcast_to(row_sums[:, None], (2 * WAVES, LANES)).astype(np.float32)
    columns = np.zeros((LANES, 2 * LANES))
    columns[:STRIDE, :81] = cosine[:, :STRIDE].T
    columns[:STRIDE, LANES : LANES + 81] = sine[:, :STRIDE].T
    columns_high, columns_low = halves(columns)
    columns_twice = np.concatenate([columns_high, columns_high], axis=0)
    weight = np.ones(81)
    weight[0] = weight[80] = 0.5
    back_columns = np.zeros((2 * LANES, PATCH_SIZE))
    back_columns[:81] = weight[:, None] * cosine
    back_columns[LANES : LANES + 81] = weight[:, None] * sine
    back_columns = halves(back_columns)
    weight = np.full(81, 2.0)
    weight[0] = weight[80] = 1.0
    back_rows = np.zeros((PATCH_SIZE, 2 * WAVES))
    back_rows[:, :81] = (weight[:, None] * cosine).T
    back_rows[:, WAVES : WAVES + 81] = -(weight[:, None] * sine).T
    back_rows = halves(back_rows)
    return (rows_both, row_sums, columns_twice, columns_low, *back_columns, *back_rows)


def fill_table(owner_ref, cell_ref, count_ref, flow_ref, table_ref):
    owners, codes = [], []
    for block in range(BLOCKS):
        for entry in range(DEST_SLOTS):
            live = entry < count_ref[0, block]
            owners.append(jnp.where(live, owner_ref[entry, block], -1))
            codes.append(BLOCKS * block + cell_ref[entry, block])

    def one(owner, carry):
        first = second = jnp.int32(-1)
        for named, code in zip(owners, codes):
            match = named == owner
            second = jnp.where(match, first, second)
            first = jnp.where(match, code, first)
        for rank, code in enumerate((first, second)):
            block = jnp.maximum(code, 0) >> 3
            base = 8 * owner + 4 * rank
            table_ref[0, base] = block
            table_ref[0, base + 1] = jnp.where(code < 0, -1, code & 7)
            table_ref[0, base + 2] = flow_ref[0, block]
            table_ref[0, base + 3] = flow_ref[1, block]
        return carry

    lax.fori_loop(0, OWNERS, one, 0)


def chunk_of(index):
    line, place = index // 8, index % 8
    holds = ((place >= 1) & (place <= 6)) | (index == 0)
    return holds, jnp.where(index == 0, CHUNKS - 1, line * 6 + place - 1)


def holder_of(chunk):
    return jnp.where(chunk == CHUNKS - 1, 0, (chunk // 6) * 8 + chunk % 6 + 1)


def chunk_at(ref, chunk, row, column):
    rows = pl.ds(pl.multiple_of(row + 16 * (chunk // 5), 16), 16)
    columns = pl.ds(pl.multiple_of(column + LANES * (chunk % 5), LANES), LANES)
    return ref.at[rows, columns]


def exchange_kernel(
    tile_ref,
    partner_ref,
    owner_ref,
    cell_ref,
    count_ref,
    flow_ref,
    own_ref,
    other_ref,
    slots_ref,
    info_ref,
    held,
    sorted_,
    mirror,
    blocks,
    outgoing,
    tables,
    fixed,
    fixed_smem,
    table_smem,
    mirror_smem,
    send_sem,
    recv_sem,
    far_sem,
    slot_sem,
    local_sem,
):
    gz, gy, gx = lax.axis_index("gz"), lax.axis_index("gy"), lax.axis_index("gx")
    half, core = gy // 2, gy % 2
    place = core * 4 + gx
    far_gy = 3 - gy
    near_gy = gy + 1 - 2 * core

    barrier = pltpu.get_barrier_semaphore()

    def greet(step, carry):
        pl.semaphore_signal(
            barrier, inc=1, device_id={"gz": lax.rem(gz + step, SECTIONS)}, device_id_type=MESH
        )
        return carry

    lax.fori_loop(1, SECTIONS, greet, 0)
    for step in range(1, 8):
        other_place = lax.rem(place + step, 8)
        pl.semaphore_signal(
            barrier,
            inc=1,
            device_id={"gy": 2 * half + other_place // 4, "gx": other_place % 4},
            device_id_type=MESH,
        )
    pl.semaphore_signal(barrier, inc=1, device_id={"gy": far_gy}, device_id_type=MESH)

    fixed[...] = jnp.round(flow_ref[...].astype(f32) * float(2**FIXED)).astype(jnp.int32)
    to_scalars = pltpu.make_async_copy(fixed, fixed_smem, local_sem)
    to_scalars.start()
    own_ref[pl.ds(HALO_ROWS, HEIGHT), pl.ds(LANES, WIDTH)] = tile_ref[...]
    top, bottom = pl.ds(0, HALO_ROWS), pl.ds(HALO_ROWS + HEIGHT, HALO_ROWS)
    left, right = pl.ds(0, LANES), pl.ds(LANES + WIDTH, LANES)
    middle = pl.ds(LANES, WIDTH)
    for ref in (own_ref, other_ref):

        @pl.when(gy == 0)
        def _():
            ref[top, middle] = jnp.zeros((HALO_ROWS, WIDTH), bf16)

        @pl.when(gy == 3)
        def _():
            ref[bottom, middle] = jnp.zeros((HALO_ROWS, WIDTH), bf16)

        @pl.when(gx == 0)
        def _():
            ref[:, left] = jnp.zeros((STRIP_ROWS, LANES), bf16)

        @pl.when(gx == 3)
        def _():
            ref[:, right] = jnp.zeros((STRIP_ROWS, LANES), bf16)

    holds, mine = chunk_of(gz)
    pl.semaphore_wait(barrier, SECTIONS - 1 + 8)

    def scatter(step, carry):
        chunk = lax.rem(mine + step, CHUNKS)
        holder = holder_of(chunk)

        @pl.when(holder != gz)
        def _():
            pltpu.make_async_remote_copy(
                src_ref=chunk_at(tile_ref, chunk, 0, 0),
                dst_ref=held.at[gz],
                send_sem=send_sem.at[0],
                recv_sem=recv_sem.at[0],
                device_id={"gz": holder},
                device_id_type=MESH,
            ).start()

        return carry

    lax.fori_loop(0, CHUNKS, scatter, 0)

    def copy(src, dst, slot, device):
        return pltpu.make_async_remote_copy(
            src_ref=src,
            dst_ref=dst,
            send_sem=far_sem.at[0, slot],
            recv_sem=far_sem.at[1, slot],
            device_id=device,
            device_id_type=MESH,
        )

    near = {"gy": near_gy}

    own_down = copy(
        tile_ref.at[pl.ds(HEIGHT - HALO_ROWS, HALO_ROWS), :], own_ref.at[top, middle], 0, near
    )
    own_up = copy(tile_ref.at[pl.ds(0, HALO_ROWS), :], own_ref.at[bottom, middle], 0, near)

    @pl.when(core == 0)
    def _():
        own_down.start()

    @pl.when(core == 1)
    def _():
        own_up.start()

    to_far = copy(tile_ref, mirror, 1, {"gy": far_gy})
    to_far.start()
    to_scalars.wait()
    fill_table(owner_ref, cell_ref, count_ref, fixed_smem, table_smem)
    to_vector = pltpu.make_async_copy(table_smem, tables.at[0], local_sem)
    to_vector.start()
    to_vector.wait()
    table_far = copy(tables.at[0], tables.at[1], 2, {"gy": far_gy})
    table_far.start()

    lane = lax.broadcasted_iota(jnp.int32, (HEIGHT, LANES), 1)

    def cut_blocks(ref, base):
        for block in range(BLOCKS):
            start = STRIDE * block
            first = start // LANES * LANES
            shift = start - first
            width = LANES if shift + STRIDE <= LANES else 2 * LANES
            window = ref[:, first : first + width].astype(f32)
            if shift:
                window = pltpu.roll(window, width - shift, 1)[:, :LANES]
            blocks[base + block] = jnp.where(lane < STRIDE, window, 0.0).astype(bf16)

    cut_blocks(tile_ref, 0)

    @pl.when(holds)
    def _():
        held[gz] = chunk_at(tile_ref, mine, 0, 0)[...]
        pltpu.make_async_copy(
            held.at[pl.ds(0, SECTIONS - 1)], held.at[pl.ds(0, SECTIONS - 1)], recv_sem.at[0]
        ).wait()

        def deliver(step, carry):
            section = lax.rem(gz + step, SECTIONS)
            sorted_[section] = held[partner_ref[0, section]]
            pltpu.make_async_remote_copy(
                src_ref=sorted_.at[section],
                dst_ref=chunk_at(other_ref, mine, HALO_ROWS, LANES),
                send_sem=send_sem.at[1],
                recv_sem=recv_sem.at[1],
                device_id={"gz": section},
                device_id_type=MESH,
            ).start()
            return carry

        lax.fori_loop(1, SECTIONS, deliver, 0)
        chunk_at(other_ref, mine, HALO_ROWS, LANES)[...] = held[partner_ref[0, gz]]

    def side_copies(ref, slot):
        to_right = copy(
            ref.at[:, pl.ds(WIDTH, LANES)], ref.at[:, left], slot, {"gx": jnp.minimum(gx + 1, 3)}
        )
        to_left = copy(
            ref.at[:, pl.ds(LANES, LANES)], ref.at[:, right], slot + 1, {"gx": jnp.maximum(gx - 1, 0)}
        )
        return to_right, to_left

    def start_sides(copies):
        @pl.when(gx < 3)
        def _():
            copies[0].start()

        @pl.when(gx > 0)
        def _():
            copies[1].start()

    def receive_sides(copies):
        @pl.when(gx > 0)
        def _():
            copies[0].wait_recv()

        @pl.when(gx < 3)
        def _():
            copies[1].wait_recv()

    def sent_sides(copies):
        @pl.when(gx < 3)
        def _():
            copies[0].wait_send()

        @pl.when(gx > 0)
        def _():
            copies[1].wait_send()

    @pl.when(core == 1)
    def _():
        own_down.wait_recv()

    @pl.when(core == 0)
    def _():
        own_up.wait_recv()

    to_far.wait_recv()

    @pl.when(gy == 1)
    def _():
        own_ref[bottom, middle] = mirror[pl.ds(0, HALO_ROWS), :]

    @pl.when(gy == 2)
    def _():
        own_ref[top, middle] = mirror[pl.ds(HEIGHT - HALO_ROWS, HALO_ROWS), :]

    own_sides = side_copies(own_ref, 3)
    start_sides(own_sides)

    table_far.wait_recv()
    fetch = pltpu.make_async_copy(tables.at[1], mirror_smem, local_sem)
    fetch.start()
    cut_blocks(mirror, BLOCKS)
    fetch.wait()

    def fill(target, index):
        owner = 8 * half + target
        for kind, table in ((0, table_smem), (1, mirror_smem)):
            for rank in range(2):
                block = table[0, 8 * owner + 4 * rank]
                index[2 * kind + rank] = blocks[BLOCKS * kind + block]

    def send_slots(step, carry):
        target = lax.rem(place + step, 8)
        fill(target, outgoing.at[target])
        device = {"gy": 2 * half + target // 4, "gx": target % 4}
        for src, dst, kind in (
            (outgoing.at[target], slots_ref.at[place], 0),
            (tables, info_ref.at[place], 1),
        ):
            pltpu.make_async_remote_copy(
                src_ref=src,
                dst_ref=dst,
                send_sem=slot_sem.at[0, kind],
                recv_sem=slot_sem.at[1, kind],
                device_id=device,
                device_id_type=MESH,
            ).start()
        return carry

    lax.fori_loop(1, 8, send_slots, 0)
    fill(place, slots_ref.at[place])
    info_ref[place] = tables[...]

    chunks = held.at[pl.ds(0, CHUNKS)]
    fewer = held.at[pl.ds(0, CHUNKS - 1)]

    @pl.when(holds)
    def _():
        pltpu.make_async_copy(fewer, fewer, recv_sem.at[1]).wait()

    @pl.when(jnp.logical_not(holds))
    def _():
        pltpu.make_async_copy(chunks, chunks, recv_sem.at[1]).wait()

    rows_up = pl.ds(HALO_ROWS, HALO_ROWS)
    rows_down = pl.ds(HEIGHT, HALO_ROWS)
    other_down = copy(
        other_ref.at[rows_down, middle], other_ref.at[top, middle], 5, {"gy": jnp.minimum(gy + 1, 3)}
    )
    other_up = copy(
        other_ref.at[rows_up, middle], other_ref.at[bottom, middle], 6, {"gy": jnp.maximum(gy - 1, 0)}
    )

    @pl.when(gy < 3)
    def _():
        other_down.start()

    @pl.when(gy > 0)
    def _():
        other_up.start()

    @pl.when(gy > 0)
    def _():
        other_down.wait_recv()

    @pl.when(gy < 3)
    def _():
        other_up.wait_recv()

    other_sides = side_copies(other_ref, 7)
    start_sides(other_sides)

    receive_sides(own_sides)
    seven = slots_ref.at[pl.ds(0, 7)]
    pltpu.make_async_copy(seven, seven, slot_sem.at[1, 0]).wait()
    seven_info = info_ref.at[pl.ds(0, 7)]
    pltpu.make_async_copy(seven_info, seven_info, slot_sem.at[1, 1]).wait()
    receive_sides(other_sides)

    pltpu.make_async_copy(seven, seven, slot_sem.at[0, 0]).wait()
    pltpu.make_async_copy(seven_info, seven_info, slot_sem.at[0, 1]).wait()

    @pl.when(holds)
    def _():
        pltpu.make_async_copy(fewer, fewer, send_sem.at[0]).wait()
        all_but_one = held.at[pl.ds(0, SECTIONS - 1)]
        pltpu.make_async_copy(all_but_one, all_but_one, send_sem.at[1]).wait()

    @pl.when(jnp.logical_not(holds))
    def _():
        pltpu.make_async_copy(chunks, chunks, send_sem.at[0]).wait()

    @pl.when(core == 0)
    def _():
        own_down.wait_send()

    @pl.when(core == 1)
    def _():
        own_up.wait_send()

    to_far.wait_send()
    table_far.wait_send()

    @pl.when(gy < 3)
    def _():
        other_down.wait_send()

    @pl.when(gy > 0)
    def _():
        other_up.wait_send()

    sent_sides(own_sides)
    sent_sides(other_sides)


def split(value):
    high = value.astype(bf16)
    return high, (value - high.astype(f32)).astype(bf16)


def dot(left, right):
    return jnp.dot(left, right, preferred_element_type=f32)


def compute_kernel(
    own_ref,
    other_ref,
    slots_ref,
    info_ref,
    mask_ref,
    *rest,
):
    tables_hbm, (correlation_hbm, warped_ref), rest = rest[:8], rest[8:10], rest[10:]
    tables_vmem, (strip, spectra, parts, cells, shifted, canvas, result, table_sem, out_sem) = (
        rest[:8],
        rest[8:],
    )
    loads = [
        pltpu.make_async_copy(src, dst, table_sem.at[index])
        for index, (src, dst) in enumerate(zip(tables_hbm, tables_vmem))
    ]
    for load in loads:
        load.start()
    (
        rows_both,
        row_sums,
        columns_twice,
        columns_low,
        back_columns_high,
        back_columns_low,
        back_rows_high,
        back_rows_low,
    ) = tables_vmem
    lane = lax.broadcasted_iota(jnp.int32, (PATCH_SIZE, LANES), 1)
    means, squares = [], []
    for index, ref in enumerate((own_ref, other_ref)):
        for block in range(HALVES):
            start = LANES - 40 + STRIDE * block
            first = start // LANES * LANES
            shift = start - first
            width = LANES if shift + STRIDE <= LANES else 2 * LANES
            window = ref[8 : 8 + PATCH_SIZE, first : first + width].astype(f32)
            window = pltpu.roll(window, width - shift, 1)[:, :LANES]
            window = jnp.where(lane < STRIDE, window, 0.0)
            mean = jnp.sum(window, keepdims=True) * (1.0 / (PATCH_SIZE * STRIDE))
            centred = jnp.where(lane < STRIDE, window - mean, 0.0)
            means.append(mean)
            squares.append(jnp.sum(centred * centred, keepdims=True))
            strip[:, pl.ds((index * HALVES + block) * LANES, LANES)] = window.astype(bf16)

    for load in loads:
        load.wait()
    levels = [sum(means[:HALVES]) * (1.0 / HALVES), sum(means[HALVES:]) * (1.0 / HALVES)]
    for block in range(2 * HALVES):
        both = dot(rows_both[...], strip[:, pl.ds(block * LANES, LANES)])
        value = both[: 2 * WAVES] + both[2 * WAVES :] - levels[block // HALVES] * row_sums[...]
        high, low = split(value)
        spectra[block, :, :LANES] = high
        spectra[block, :, LANES:] = low
    for block in range(2 * HALVES):
        parts[block] = dot(spectra[block], columns_twice[...]) + dot(
            spectra[block, :, :LANES], columns_low[...]
        )

    row = lax.broadcasted_iota(jnp.int32, (WAVES, LANES), 0)
    column = lax.broadcasted_iota(jnp.int32, (WAVES, LANES), 1)
    constant = (row == 0) & (column == 0)
    odd = column % 2 == 1
    count = PATCH_SIZE * STRIDE

    def spectrum(first):
        def one(rows, lanes):
            later = parts[first + 1, rows, lanes]
            return parts[first, rows, lanes] + jnp.where(odd, -later, later)

        upper, lower = pl.ds(0, WAVES), pl.ds(WAVES, WAVES)
        low, high = pl.ds(0, LANES), pl.ds(LANES, LANES)
        a = jnp.where(constant, 0.0, one(upper, low))
        return a, one(lower, high), one(lower, low), one(upper, high)

    stores = []
    for patch in range(PATCH_COLS):
        scale = mask_ref[0, patch].astype(f32) * (1.0 / PATCH_SIZE**3)
        for base in (0, HALVES):
            first, second = base + patch, base + patch + 1
            gap = means[first] - means[second]
            spread = (squares[first] + squares[second] + gap * gap * (count / 2)) * (0.5 / count)
            scale = scale / jnp.sqrt(spread + epsilon)
        a, b, c, d = spectrum(patch)
        e, f, g, h = spectrum(HALVES + patch)
        scale = 2.0 * scale
        even_real = (a * e + b * f + c * g + d * h) * scale
        odd_real = (c * h + d * g - a * f - b * e) * scale
        even_imag = (c * e - d * f - a * g + b * h) * scale
        odd_imag = (d * e - c * f - a * h + b * g) * scale
        joined = jnp.concatenate(
            [
                jnp.concatenate([even_real, -odd_imag], axis=1),
                jnp.concatenate([even_imag, odd_real], axis=1),
            ],
            axis=0,
        )
        high, low = split(joined)
        half = (
            dot(high, back_columns_high[...])
            + dot(low, back_columns_high[...])
            + dot(high, back_columns_low[...])
        )
        high, low = split(half)
        result[patch] = (
            dot(back_rows_high[...], high)
            + dot(back_rows_high[...], low)
            + dot(back_rows_low[...], high)
        )
        stores.append(
            pltpu.make_async_copy(result.at[patch], correlation_hbm.at[patch], out_sem.at[patch])
        )
        stores[-1].start()

    cells[...] = jnp.zeros_like(cells)
    shifted[...] = jnp.zeros_like(shifted)
    mine = (lax.axis_index("gy") * 4 + lax.axis_index("gx")) * 8

    def entry(index, carry):
        source, kind, rank = index // 4, index % 4 // 2, index % 2
        base = mine + 4 * rank
        cell = info_ref[source, kind, 0, base + 1]

        @pl.when(cell >= 0)
        def _():
            down, across = info_ref[source, kind, 0, base + 2], info_ref[source, kind, 0, base + 3]
            whole_down, whole_across = down >> FIXED, across >> FIXED
            unit = 1.0 / 2**FIXED
            part_down = (down & (2**FIXED - 1)).astype(f32) * unit
            part_across = (across & (2**FIXED - 1)).astype(f32) * unit
            block = slots_ref[source, 2 * kind + rank].astype(f32)
            here = pltpu.roll(block, whole_across + MARGIN, 1)
            after = pltpu.roll(block, whole_across + MARGIN + 1, 1)
            shifted[pl.ds(MARGIN, HEIGHT), :] = here * (1.0 - part_across) + after * part_across
            here = shifted[pl.ds(MARGIN - whole_down, HEIGHT), :]
            after = shifted[pl.ds(MARGIN - 1 - whole_down, HEIGHT), :]
            value = here * (1.0 - part_down) + after * part_down
            cells[cell] = cells[cell] + value.astype(bf16).astype(f32)

        return carry

    lax.fori_loop(0, 32, entry, 0)
    canvas[...] = jnp.zeros_like(canvas)
    for cell in range(BLOCKS):
        start = LANES - MARGIN + STRIDE * cell
        first = start // LANES * LANES
        shift = start - first
        wide = jnp.concatenate([cells[cell], jnp.zeros((HEIGHT, LANES), f32)], axis=1)
        if shift:
            wide = pltpu.roll(wide, shift, 1)
        canvas[:, first : first + 2 * LANES] = canvas[:, first : first + 2 * LANES] + wide
    warped_ref[...] = canvas[:, LANES : LANES + WIDTH]
    for store in stores:
        store.wait()


VMEM = pl.BlockSpec(memory_space=pltpu.VMEM)
SMEM = pl.BlockSpec(memory_space=pltpu.SMEM)
ANY = pl.BlockSpec(memory_space=pl.ANY)


def body(tables, images, partner, patch_mask, flows, dest_count, dest_owner, dest_cell):
    tile = images[0]
    own, other, slots, info = pl.pallas_call(
        exchange_kernel,
        out_shape=[
            jax.ShapeDtypeStruct((STRIP_ROWS, STRIP_COLS), bf16),
            jax.ShapeDtypeStruct((STRIP_ROWS, STRIP_COLS), bf16),
            jax.ShapeDtypeStruct((8, 4, HEIGHT, LANES), bf16),
            jax.ShapeDtypeStruct((8, 2, 1, 128), jnp.int32),
        ],
        in_specs=[VMEM, SMEM, SMEM, SMEM, SMEM, VMEM],
        out_specs=[VMEM] * 4,
        scratch_shapes=[
            pltpu.VMEM((SECTIONS, 16, LANES), bf16),
            pltpu.VMEM((SECTIONS, 16, LANES), bf16),
            pltpu.VMEM((HEIGHT, WIDTH), bf16),
            pltpu.VMEM((2 * BLOCKS, HEIGHT, LANES), bf16),
            pltpu.VMEM((8, 4, HEIGHT, LANES), bf16),
            pltpu.VMEM((2, 1, 128), jnp.int32),
            pltpu.VMEM((2, BLOCKS), jnp.int32),
            pltpu.SMEM((2, BLOCKS), jnp.int32),
            pltpu.SMEM((1, 128), jnp.int32),
            pltpu.SMEM((1, 128), jnp.int32),
            pltpu.SemaphoreType.DMA((2,)),
            pltpu.SemaphoreType.DMA((2,)),
            pltpu.SemaphoreType.DMA((2, 9)),
            pltpu.SemaphoreType.DMA((2, 2)),
            pltpu.SemaphoreType.DMA,
        ],
        compiler_params=pltpu.CompilerParams(
            collective_id=0, has_side_effects=True, vmem_limit_bytes=VMEM_BYTES
        ),
    )(
        tile,
        partner[0],
        dest_owner[0, 0, 0].T,
        dest_cell[0, 0, 0].T,
        dest_count[0, 0],
        flows[0, 0, 0].T,
    )
    correlation, warped = pl.pallas_call(
        compute_kernel,
        out_shape=[
            jax.ShapeDtypeStruct((PATCH_COLS, PATCH_SIZE, PATCH_SIZE), f32),
            jax.ShapeDtypeStruct((HEIGHT, WIDTH), f32),
        ],
        in_specs=[VMEM, VMEM, VMEM, SMEM, SMEM] + [ANY] * 8,
        out_specs=[ANY, VMEM],
        scratch_shapes=[pltpu.VMEM(table.shape, table.dtype) for table in tables]
        + [
            pltpu.VMEM((PATCH_SIZE, 2 * HALVES * LANES), bf16),
            pltpu.VMEM((2 * HALVES, 2 * WAVES, 2 * LANES), bf16),
            pltpu.VMEM((2 * HALVES, 2 * WAVES, 2 * LANES), f32),
            pltpu.VMEM((BLOCKS, HEIGHT, LANES), f32),
            pltpu.VMEM((128, LANES), f32),
            pltpu.VMEM((HEIGHT, STRIP_COLS), f32),
            pltpu.VMEM((PATCH_COLS, PATCH_SIZE, PATCH_SIZE), f32),
            pltpu.SemaphoreType.DMA((8,)),
            pltpu.SemaphoreType.DMA((PATCH_COLS,)),
        ],
        compiler_params=pltpu.CompilerParams(vmem_limit_bytes=VMEM_BYTES),
    )(own, other, slots, info, patch_mask[0], *tables)
    return correlation[None, None], warped[None]


def solution(mesh):
    placed = (
        P("gz", "gy", "gx"),
        P("gy", "gx", None),
        P("gz", "gy", "gx"),
        P("gz", "gy", "gx", None, None),
        P("gz", "gy", "gx", None),
        P("gz", "gy", "gx", None, None),
        P("gz", "gy", "gx", None, None),
    )
    tables = tuple(jnp.asarray(table) for table in make_tables())
    return jax.shard_map(
        functools.partial(body, tables),
        mesh=mesh,
        in_specs=placed,
        out_specs=(P("gz", "gy", "gx", None, None), P("gz", "gy", "gx")),
        check_vma=False,
    )
```

```python
import functools

import jax
import jax.numpy as jnp
import ml_dtypes
import numpy as np
from jax import lax
from jax.experimental import pallas as pl
from jax.experimental.pallas import tpu as pltpu
from jax.sharding import PartitionSpec as P

PATCH_SIZE = 160
STRIDE = 80
PATCH_COLS = 8
MARGIN = 24
DEST_SLOTS = 2
BLOCKS = 8
OWNERS = 16
PADDED = 128
SECTIONS = 32
HEIGHT = 80
WIDTH = 640
CHUNKS = 25
LANES = 128
HALO_ROWS = 48
STRIP_ROWS = HEIGHT + 2 * HALO_ROWS
STRIP_COLS = WIDTH + 2 * LANES
HALVES = 9
WAVES = 88
VMEM_BYTES = 60 * 2**20
FIXED = 24

epsilon = 1e-05
f32 = jnp.float32
bf16 = jnp.bfloat16
MESH = pl.DeviceIdType.MESH


def halves(table):
    high = table.astype(ml_dtypes.bfloat16)
    low = (table - high.astype(np.float64)).astype(ml_dtypes.bfloat16)
    return high, low


def make_tables():
    wave = np.arange(81)
    place = np.arange(PATCH_SIZE)
    angle = 2.0 * np.pi * (np.outer(wave, place) % PATCH_SIZE) / PATCH_SIZE
    cosine, sine = np.cos(angle), np.sin(angle)
    sine[0] = 0.0
    sine[80] = 0.0
    rows = np.zeros((2 * WAVES, PATCH_SIZE))
    rows[:81] = cosine
    rows[WAVES : WAVES + 81] = sine
    rows_high, rows_low = halves(rows)
    rows_both = np.concatenate([rows_high, rows_low], axis=0)
    row_sums = (rows_high.astype(np.float64) + rows_low.astype(np.float64)).sum(axis=1)
    row_sums = np.broadcast_to(row_sums[:, None], (2 * WAVES, LANES)).astype(np.float32)
    columns = np.zeros((LANES, 2 * LANES))
    columns[:STRIDE, :81] = cosine[:, :STRIDE].T
    columns[:STRIDE, LANES : LANES + 81] = sine[:, :STRIDE].T
    columns_high, columns_low = halves(columns)
    columns_twice = np.concatenate([columns_high, columns_high], axis=0)
    weight = np.ones(81)
    weight[0] = weight[80] = 0.5
    back_columns = np.zeros((2 * LANES, PATCH_SIZE))
    back_columns[:81] = weight[:, None] * cosine
    back_columns[LANES : LANES + 81] = weight[:, None] * sine
    back_columns = halves(back_columns)
    weight = np.full(81, 2.0)
    weight[0] = weight[80] = 1.0
    back_rows = np.zeros((PATCH_SIZE, 2 * WAVES))
    back_rows[:, :81] = (weight[:, None] * cosine).T
    back_rows[:, WAVES : WAVES + 81] = -(weight[:, None] * sine).T
    back_rows = halves(back_rows)
    return (rows_both, row_sums, columns_twice, columns_low, *back_columns, *back_rows)


def fill_table(owner_ref, cell_ref, count_ref, flow_ref, table_ref):
    owners, codes = [], []
    for block in range(BLOCKS):
        for entry in range(DEST_SLOTS):
            live = entry < count_ref[0, block]
            owners.append(jnp.where(live, owner_ref[entry, block], -1))
            codes.append(BLOCKS * block + cell_ref[entry, block])

    def one(owner, carry):
        first = second = jnp.int32(-1)
        for named, code in zip(owners, codes):
            match = named == owner
            second = jnp.where(match, first, second)
            first = jnp.where(match, code, first)
        for rank, code in enumerate((first, second)):
            block = jnp.maximum(code, 0) >> 3
            base = 8 * owner + 4 * rank
            table_ref[0, base] = block
            table_ref[0, base + 1] = jnp.where(code < 0, -1, code & 7)
            table_ref[0, base + 2] = flow_ref[0, block]
            table_ref[0, base + 3] = flow_ref[1, block]
        return carry

    lax.fori_loop(0, OWNERS, one, 0)


def chunk_of(index):
    line, place = index // 8, index % 8
    holds = ((place >= 1) & (place <= 6)) | (index == 0)
    return holds, jnp.where(index == 0, CHUNKS - 1, line * 6 + place - 1)


def holder_of(chunk):
    return jnp.where(chunk == CHUNKS - 1, 0, (chunk // 6) * 8 + chunk % 6 + 1)


def chunk_at(ref, chunk, row, column):
    rows = pl.ds(pl.multiple_of(row + 16 * (chunk // 5), 16), 16)
    columns = pl.ds(pl.multiple_of(column + LANES * (chunk % 5), LANES), LANES)
    return ref.at[rows, columns]


def exchange_kernel(
    tile_ref,
    partner_ref,
    owner_ref,
    cell_ref,
    count_ref,
    flow_ref,
    *rest,
):
    tables_hbm, (other_ref, parts_hbm, warped_hbm, scale_ref), rest = rest[:4], rest[4:8], rest[8:]
    tables_vmem, rest = rest[:4], rest[4:]
    (
        own_ref,
        slots_ref,
        info_ref,
        info_smem,
        held,
        sorted_,
        mirror,
        blocks,
        outgoing,
        tables,
        fixed,
        fixed_smem,
        table_smem,
        mirror_smem,
        strip,
        spectra,
        parts,
        cells,
        shifted,
        canvas,
        warped,
        send_sem,
        recv_sem,
        far_sem,
        slot_sem,
        local_sem,
        table_sem,
        out_sem,
    ) = rest
    gz, gy, gx = lax.axis_index("gz"), lax.axis_index("gy"), lax.axis_index("gx")
    half, core = gy // 2, gy % 2
    place = core * 4 + gx
    far_gy = 3 - gy
    near_gy = gy + 1 - 2 * core

    barrier = pltpu.get_barrier_semaphore()

    def greet(step, carry):
        pl.semaphore_signal(
            barrier, inc=1, device_id={"gz": lax.rem(gz + step, SECTIONS)}, device_id_type=MESH
        )
        return carry

    pl.semaphore_signal(barrier, inc=1, device_id={"gy": far_gy}, device_id_type=MESH)
    lax.fori_loop(1, SECTIONS, greet, 0)
    for step in range(1, 8):
        other_place = lax.rem(place + step, 8)
        pl.semaphore_signal(
            barrier,
            inc=1,
            device_id={"gy": 2 * half + other_place // 4, "gx": other_place % 4},
            device_id_type=MESH,
        )

    loads = [
        pltpu.make_async_copy(src, dst, table_sem.at[index])
        for index, (src, dst) in enumerate(zip(tables_hbm, tables_vmem))
    ]
    for load in loads:
        load.start()
    fixed[...] = jnp.round(flow_ref[...].astype(f32) * float(2**FIXED)).astype(jnp.int32)
    to_scalars = pltpu.make_async_copy(fixed, fixed_smem, local_sem)
    to_scalars.start()
    own_ref[pl.ds(HALO_ROWS, HEIGHT), pl.ds(LANES, WIDTH)] = tile_ref[...]
    top, bottom = pl.ds(0, HALO_ROWS), pl.ds(HALO_ROWS + HEIGHT, HALO_ROWS)
    left, right = pl.ds(0, LANES), pl.ds(LANES + WIDTH, LANES)
    middle = pl.ds(LANES, WIDTH)
    for ref in (own_ref, other_ref):

        @pl.when(gy == 0)
        def _():
            ref[top, middle] = jnp.zeros((HALO_ROWS, WIDTH), bf16)

        @pl.when(gy == 3)
        def _():
            ref[bottom, middle] = jnp.zeros((HALO_ROWS, WIDTH), bf16)

        @pl.when(gx == 0)
        def _():
            ref[:, left] = jnp.zeros((STRIP_ROWS, LANES), bf16)

        @pl.when(gx == 3)
        def _():
            ref[:, right] = jnp.zeros((STRIP_ROWS, LANES), bf16)

    lane = lax.broadcasted_iota(jnp.int32, (HEIGHT, LANES), 1)

    def cut_blocks(ref, base):
        for block in range(BLOCKS):
            start = STRIDE * block
            first = start // LANES * LANES
            shift = start - first
            width = LANES if shift + STRIDE <= LANES else 2 * LANES
            window = ref[:, first : first + width].astype(f32)
            if shift:
                window = pltpu.roll(window, width - shift, 1)[:, :LANES]
            blocks[base + block] = jnp.where(lane < STRIDE, window, 0.0).astype(bf16)

    def fill(kind, table):
        for target in range(8):
            base = 8 * (8 * half + target)
            for rank in range(2):
                block = table[0, base + 4 * rank]
                outgoing[kind, target, rank] = blocks[BLOCKS * kind + block]

    cut_blocks(tile_ref, 0)
    to_scalars.wait()
    fill_table(owner_ref, cell_ref, count_ref, fixed_smem, table_smem)
    to_vector = pltpu.make_async_copy(table_smem, tables.at[0], local_sem)
    to_vector.start()
    fill(0, table_smem)
    to_vector.wait()
    holds, mine = chunk_of(gz)
    pl.semaphore_wait(barrier, SECTIONS - 1 + 8)

    def scatter(step, carry):
        chunk = lax.rem(mine + step, CHUNKS)
        holder = holder_of(chunk)

        @pl.when(holder != gz)
        def _():
            pltpu.make_async_remote_copy(
                src_ref=chunk_at(tile_ref, chunk, 0, 0),
                dst_ref=held.at[gz],
                send_sem=send_sem.at[0],
                recv_sem=recv_sem.at[0],
                device_id={"gz": holder},
                device_id_type=MESH,
            ).start()

        return carry

    def copy(src, dst, slot, device):
        return pltpu.make_async_remote_copy(
            src_ref=src,
            dst_ref=dst,
            send_sem=far_sem.at[0, slot],
            recv_sem=far_sem.at[1, slot],
            device_id=device,
            device_id_type=MESH,
        )

    near = {"gy": near_gy}
    own_down = copy(
        tile_ref.at[pl.ds(HEIGHT - HALO_ROWS, HALO_ROWS), :], own_ref.at[top, middle], 0, near
    )
    own_up = copy(tile_ref.at[pl.ds(0, HALO_ROWS), :], own_ref.at[bottom, middle], 0, near)
    to_far = copy(tile_ref, mirror, 1, {"gy": far_gy})
    table_far = copy(tables.at[0], tables.at[1], 2, {"gy": far_gy})

    def send_slots(kind):
        def one(step, carry):
            target = lax.rem(place + step, 8)
            device = {"gy": 2 * half + target // 4, "gx": target % 4}
            for src, dst, row in (
                (outgoing.at[kind, target], slots_ref.at[kind, place], 0),
                (tables.at[kind], info_ref.at[kind, place], 1),
            ):
                pltpu.make_async_remote_copy(
                    src_ref=src,
                    dst_ref=dst,
                    send_sem=slot_sem.at[0, kind, row],
                    recv_sem=slot_sem.at[1, kind, row],
                    device_id=device,
                    device_id_type=MESH,
                ).start()
            return carry

        lax.fori_loop(1, 8, one, 0)
        slots_ref[kind, place] = outgoing[kind, place]
        info_ref[kind, place] = tables[kind]

    table_far.start()
    to_far.start()
    lax.fori_loop(0, CHUNKS, scatter, 0)

    @pl.when(core == 0)
    def _():
        own_down.start()

    @pl.when(core == 1)
    def _():
        own_up.start()

    send_slots(0)

    @pl.when(holds)
    def _():
        held[gz] = chunk_at(tile_ref, mine, 0, 0)[...]
        pltpu.make_async_copy(
            held.at[pl.ds(0, SECTIONS - 1)], held.at[pl.ds(0, SECTIONS - 1)], recv_sem.at[0]
        ).wait()
        for section in range(SECTIONS):
            sorted_[section] = held[partner_ref[0, section]]

        def deliver(step, carry):
            section = lax.rem(gz + step, SECTIONS)
            pltpu.make_async_remote_copy(
                src_ref=sorted_.at[section],
                dst_ref=chunk_at(other_ref, mine, HALO_ROWS, LANES),
                send_sem=send_sem.at[1],
                recv_sem=recv_sem.at[1],
                device_id={"gz": section},
                device_id_type=MESH,
            ).start()
            return carry

        lax.fori_loop(1, SECTIONS, deliver, 0)
        chunk_at(other_ref, mine, HALO_ROWS, LANES)[...] = sorted_[gz]


    def side_copies(ref, slot):
        to_right = copy(
            ref.at[:, pl.ds(WIDTH, LANES)], ref.at[:, left], slot, {"gx": jnp.minimum(gx + 1, 3)}
        )
        to_left = copy(
            ref.at[:, pl.ds(LANES, LANES)], ref.at[:, right], slot + 1, {"gx": jnp.maximum(gx - 1, 0)}
        )
        return to_right, to_left

    def start_sides(copies):
        @pl.when(gx < 3)
        def _():
            copies[0].start()

        @pl.when(gx > 0)
        def _():
            copies[1].start()

    def receive_sides(copies):
        @pl.when(gx > 0)
        def _():
            copies[0].wait_recv()

        @pl.when(gx < 3)
        def _():
            copies[1].wait_recv()

    def sent_sides(copies):
        @pl.when(gx < 3)
        def _():
            copies[0].wait_send()

        @pl.when(gx > 0)
        def _():
            copies[1].wait_send()

    chunks = held.at[pl.ds(0, CHUNKS)]
    fewer = held.at[pl.ds(0, CHUNKS - 1)]
    rows_up = pl.ds(HALO_ROWS, HALO_ROWS)
    rows_down = pl.ds(HEIGHT, HALO_ROWS)
    other_down = copy(
        other_ref.at[rows_down, middle], other_ref.at[top, middle], 5, {"gy": jnp.minimum(gy + 1, 3)}
    )
    other_up = copy(
        other_ref.at[rows_up, middle], other_ref.at[bottom, middle], 6, {"gy": jnp.maximum(gy - 1, 0)}
    )
    other_sides = side_copies(other_ref, 7)
    own_sides = side_copies(own_ref, 3)

    def pass_rows():
        @pl.when(holds)
        def _():
            pltpu.make_async_copy(fewer, fewer, recv_sem.at[1]).wait()

        @pl.when(jnp.logical_not(holds))
        def _():
            pltpu.make_async_copy(chunks, chunks, recv_sem.at[1]).wait()

        @pl.when(gy < 3)
        def _():
            other_down.start()

        @pl.when(gy > 0)
        def _():
            other_up.start()

    def pass_columns():
        @pl.when(gy > 0)
        def _():
            other_down.wait_recv()

        @pl.when(gy < 3)
        def _():
            other_up.wait_recv()

        start_sides(other_sides)

    def take_mirror():
        @pl.when(core == 1)
        def _():
            own_down.wait_recv()

        @pl.when(core == 0)
        def _():
            own_up.wait_recv()

        table_far.wait_recv()
        fetch = pltpu.make_async_copy(tables.at[1], mirror_smem, local_sem)
        fetch.start()
        to_far.wait_recv()

        @pl.when(gy == 1)
        def _():
            own_ref[bottom, middle] = mirror[pl.ds(0, HALO_ROWS), :]

        @pl.when(gy == 2)
        def _():
            own_ref[top, middle] = mirror[pl.ds(HEIGHT - HALO_ROWS, HALO_ROWS), :]

        start_sides(own_sides)
        cut_blocks(mirror, BLOCKS)
        fetch.wait()
        fill(1, mirror_smem)
        send_slots(1)

    stores = [
        pltpu.make_async_copy(parts, parts_hbm, out_sem.at[0]),
        pltpu.make_async_copy(warped, warped_hbm, out_sem.at[1]),
    ]

    def own_spectra():
        receive_sides(own_sides)
        for load in loads:
            load.wait()
        scales = forward(own_ref, strip, spectra, parts, *tables_vmem)
        stores[0].start()
        for patch, scale in enumerate(scales):
            scale_ref[patch : patch + 1, :] = jnp.broadcast_to(scale, (1, LANES))

    def warp():
        for kind in range(2):
            seven, seven_info = slots_ref.at[kind, pl.ds(0, 7)], info_ref.at[kind, pl.ds(0, 7)]
            pltpu.make_async_copy(seven, seven, slot_sem.at[1, kind, 0]).wait()
            pltpu.make_async_copy(seven_info, seven_info, slot_sem.at[1, kind, 1]).wait()
        fetch = pltpu.make_async_copy(info_ref, info_smem, local_sem)
        fetch.start()
        cells[...] = jnp.zeros_like(cells)
        shifted[...] = jnp.zeros_like(shifted)
        fetch.wait()
        add_up(slots_ref, info_smem, 8 * (4 * gy + gx), cells, shifted, canvas, warped)
        stores[1].start()

    take_mirror()
    own_spectra()
    pass_rows()
    warp()
    pass_columns()
    receive_sides(other_sides)

    for kind in range(2):
        seven, seven_info = slots_ref.at[kind, pl.ds(0, 7)], info_ref.at[kind, pl.ds(0, 7)]
        pltpu.make_async_copy(seven, seven, slot_sem.at[0, kind, 0]).wait()
        pltpu.make_async_copy(seven_info, seven_info, slot_sem.at[0, kind, 1]).wait()

    @pl.when(holds)
    def _():
        pltpu.make_async_copy(fewer, fewer, send_sem.at[0]).wait()
        all_but_one = held.at[pl.ds(0, SECTIONS - 1)]
        pltpu.make_async_copy(all_but_one, all_but_one, send_sem.at[1]).wait()

    @pl.when(jnp.logical_not(holds))
    def _():
        pltpu.make_async_copy(chunks, chunks, send_sem.at[0]).wait()

    @pl.when(core == 0)
    def _():
        own_down.wait_send()

    @pl.when(core == 1)
    def _():
        own_up.wait_send()

    to_far.wait_send()
    table_far.wait_send()

    @pl.when(gy < 3)
    def _():
        other_down.wait_send()

    @pl.when(gy > 0)
    def _():
        other_up.wait_send()

    sent_sides(own_sides)
    sent_sides(other_sides)
    for store in stores:
        store.wait()


def split(value):
    high = value.astype(bf16)
    return high, (value - high.astype(f32)).astype(bf16)


def dot(left, right):
    return jnp.dot(left, right, preferred_element_type=f32)


def forward(ref, strip, spectra, parts, rows_both, row_sums, columns_twice, columns_low):
    lane = lax.broadcasted_iota(jnp.int32, (PATCH_SIZE, LANES), 1)
    means, squares = [], []
    for block in range(HALVES):
        start = LANES - 40 + STRIDE * block
        first = start // LANES * LANES
        shift = start - first
        width = LANES if shift + STRIDE <= LANES else 2 * LANES
        window = ref[8 : 8 + PATCH_SIZE, first : first + width].astype(f32)
        window = pltpu.roll(window, width - shift, 1)[:, :LANES]
        window = jnp.where(lane < STRIDE, window, 0.0)
        mean = jnp.sum(window, keepdims=True) * (1.0 / (PATCH_SIZE * STRIDE))
        centred = jnp.where(lane < STRIDE, window - mean, 0.0)
        means.append(mean)
        squares.append(jnp.sum(centred * centred, keepdims=True))
        strip[:, pl.ds(block * LANES, LANES)] = window.astype(bf16)

    level = sum(means) * (1.0 / HALVES) * row_sums[...]
    for block in range(HALVES):
        both = dot(rows_both[...], strip[:, pl.ds(block * LANES, LANES)])
        value = both[: 2 * WAVES] + both[2 * WAVES :] - level
        high, low = split(value)
        spectra[block, :, :LANES] = high
        spectra[block, :, LANES:] = low
    for block in range(HALVES):
        parts[block] = dot(spectra[block], columns_twice[...]) + dot(
            spectra[block, :, :LANES], columns_low[...]
        )

    count = PATCH_SIZE * STRIDE
    scales = []
    for patch in range(PATCH_COLS):
        gap = means[patch] - means[patch + 1]
        spread = (squares[patch] + squares[patch + 1] + gap * gap * (count / 2)) * (0.5 / count)
        scales.append(1.0 / jnp.sqrt(spread + epsilon))
    return scales


def add_up(slots_ref, info_smem, mine, cells, shifted, canvas, warped):
    unit = 1.0 / 2**FIXED

    def entries(source, carry):
        values, named = [], []
        for kind in range(2):
            for rank in range(2):
                base = mine + 4 * rank
                named.append(info_smem[kind, source, 0, base + 1])
                down = info_smem[kind, source, 0, base + 2]
                across = info_smem[kind, source, 0, base + 3]
                whole_down = jnp.clip(down >> FIXED, 1 - MARGIN, MARGIN - 1)
                whole_across = jnp.clip(across >> FIXED, 1 - MARGIN, MARGIN - 1)
                part_down = (down & (2**FIXED - 1)).astype(f32) * unit
                part_across = (across & (2**FIXED - 1)).astype(f32) * unit
                block = slots_ref[kind, source, rank].astype(f32)
                here = pltpu.roll(block, whole_across + MARGIN, 1)
                after = pltpu.roll(here, 1, 1)
                room = shifted.at[2 * kind + rank]
                room[pl.ds(MARGIN, HEIGHT), :] = here * (1.0 - part_across) + after * part_across
                here = room[pl.ds(MARGIN - whole_down, HEIGHT), :]
                after = room[pl.ds(MARGIN - 1 - whole_down, HEIGHT), :]
                value = here * (1.0 - part_down) + after * part_down
                values.append(value.astype(bf16).astype(f32))
        for cell in range(BLOCKS):
            total = cells[cell]
            for value, name in zip(values, named):
                total = total + value * (name == cell).astype(f32)
            cells[cell] = total
        return carry

    lax.fori_loop(0, 8, entries, 0)
    canvas[...] = jnp.zeros_like(canvas)
    for cell in range(BLOCKS):
        start = LANES - MARGIN + STRIDE * cell
        first = start // LANES * LANES
        shift = start - first
        wide = jnp.concatenate([cells[cell], jnp.zeros((HEIGHT, LANES), f32)], axis=1)
        if shift:
            wide = pltpu.roll(wide, shift, 1)
        canvas[:, first : first + 2 * LANES] = canvas[:, first : first + 2 * LANES] + wide
    warped[...] = canvas[:, LANES : LANES + WIDTH]


def compute_kernel(other_ref, parts_hbm, warped_in, scale_ref, mask_ref, *rest):
    tables_hbm, (correlation_hbm, warped_hbm), rest = rest[:8], rest[8:10], rest[10:]
    tables_vmem, rest = rest[:8], rest[8:]
    strip, spectra, own_parts, parts, result, table_sem, part_sem, out_sem = rest
    loads = [
        pltpu.make_async_copy(src, dst, table_sem.at[index])
        for index, (src, dst) in enumerate(zip(tables_hbm, tables_vmem))
    ]
    for load in loads:
        load.start()
    own_load = pltpu.make_async_copy(parts_hbm, own_parts, part_sem)
    own_load.start()
    stores = [pltpu.make_async_copy(warped_in, warped_hbm, out_sem.at[PATCH_COLS])]
    stores[0].start()
    back_columns_high, back_columns_low, back_rows_high, back_rows_low = tables_vmem[4:]
    for load in loads:
        load.wait()
    scales = forward(other_ref, strip, spectra, parts, *tables_vmem[:4])
    own_load.wait()

    row = lax.broadcasted_iota(jnp.int32, (WAVES, LANES), 0)
    column = lax.broadcasted_iota(jnp.int32, (WAVES, LANES), 1)
    constant = (row == 0) & (column == 0)
    odd = column % 2 == 1

    def spectrum(ref, first):
        def one(rows, lanes):
            later = ref[first + 1, rows, lanes]
            return ref[first, rows, lanes] + jnp.where(odd, -later, later)

        upper, lower = pl.ds(0, WAVES), pl.ds(WAVES, WAVES)
        low, high = pl.ds(0, LANES), pl.ds(LANES, LANES)
        a = jnp.where(constant, 0.0, one(upper, low))
        return a, one(lower, high), one(lower, low), one(upper, high)

    for patch in range(PATCH_COLS):
        scale = mask_ref[0, patch].astype(f32) * (2.0 / PATCH_SIZE**3)
        scale = scale * scales[patch] * scale_ref[patch : patch + 1, :]
        a, b, c, d = spectrum(own_parts, patch)
        e, f, g, h = spectrum(parts, patch)
        even_real = (a * e + b * f + c * g + d * h) * scale
        odd_real = (c * h + d * g - a * f - b * e) * scale
        even_imag = (c * e - d * f - a * g + b * h) * scale
        odd_imag = (d * e - c * f - a * h + b * g) * scale
        joined = jnp.concatenate(
            [
                jnp.concatenate([even_real, -odd_imag], axis=1),
                jnp.concatenate([even_imag, odd_real], axis=1),
            ],
            axis=0,
        )
        high, low = split(joined)
        half = (
            dot(high, back_columns_high[...])
            + dot(low, back_columns_high[...])
            + dot(high, back_columns_low[...])
        )
        high, low = split(half)
        result[patch] = (
            dot(back_rows_high[...], high)
            + dot(back_rows_high[...], low)
            + dot(back_rows_low[...], high)
        )
        stores.append(
            pltpu.make_async_copy(result.at[patch], correlation_hbm.at[patch], out_sem.at[patch])
        )
        stores[-1].start()
    for store in stores:
        store.wait()


VMEM = pl.BlockSpec(memory_space=pltpu.VMEM)
SMEM = pl.BlockSpec(memory_space=pltpu.SMEM)
ANY = pl.BlockSpec(memory_space=pl.ANY)


def body(tables, images, partner, patch_mask, flows, dest_count, dest_owner, dest_cell):
    space = [pltpu.VMEM(table.shape, table.dtype) for table in tables]
    parts_shape = (HALVES, 2 * WAVES, 2 * LANES)
    other, parts, warped, scale = pl.pallas_call(
        exchange_kernel,
        out_shape=[
            jax.ShapeDtypeStruct((STRIP_ROWS, STRIP_COLS), bf16),
            jax.ShapeDtypeStruct(parts_shape, f32),
            jax.ShapeDtypeStruct((HEIGHT, WIDTH), f32),
            jax.ShapeDtypeStruct((PATCH_COLS, LANES), f32),
        ],
        in_specs=[VMEM, SMEM, SMEM, SMEM, SMEM, VMEM] + [ANY] * 4,
        out_specs=[VMEM, ANY, ANY, VMEM],
        scratch_shapes=space[:4]
        + [
            pltpu.VMEM((STRIP_ROWS, STRIP_COLS), bf16),
            pltpu.VMEM((2, 8, 2, HEIGHT, LANES), bf16),
            pltpu.VMEM((2, 8, 1, 128), jnp.int32),
            pltpu.SMEM((2, 8, 1, 128), jnp.int32),
            pltpu.VMEM((SECTIONS, 16, LANES), bf16),
            pltpu.VMEM((SECTIONS, 16, LANES), bf16),
            pltpu.VMEM((HEIGHT, WIDTH), bf16),
            pltpu.VMEM((2 * BLOCKS, HEIGHT, LANES), bf16),
            pltpu.VMEM((2, 8, 2, HEIGHT, LANES), bf16),
            pltpu.VMEM((2, 1, 128), jnp.int32),
            pltpu.VMEM((2, BLOCKS), jnp.int32),
            pltpu.SMEM((2, BLOCKS), jnp.int32),
            pltpu.SMEM((1, 128), jnp.int32),
            pltpu.SMEM((1, 128), jnp.int32),
            pltpu.VMEM((PATCH_SIZE, HALVES * LANES), bf16),
            pltpu.VMEM(parts_shape, bf16),
            pltpu.VMEM(parts_shape, f32),
            pltpu.VMEM((BLOCKS, HEIGHT, LANES), f32),
            pltpu.VMEM((4, 128, LANES), f32),
            pltpu.VMEM((HEIGHT, STRIP_COLS), f32),
            pltpu.VMEM((HEIGHT, WIDTH), f32),
            pltpu.SemaphoreType.DMA((2,)),
            pltpu.SemaphoreType.DMA((2,)),
            pltpu.SemaphoreType.DMA((2, 9)),
            pltpu.SemaphoreType.DMA((2, 2, 2)),
            pltpu.SemaphoreType.DMA,
            pltpu.SemaphoreType.DMA((4,)),
            pltpu.SemaphoreType.DMA((2,)),
        ],
        compiler_params=pltpu.CompilerParams(
            collective_id=0, has_side_effects=True, vmem_limit_bytes=VMEM_BYTES
        ),
    )(
        images[0],
        partner[0],
        dest_owner[0, 0, 0].T,
        dest_cell[0, 0, 0].T,
        dest_count[0, 0],
        flows[0, 0, 0].T,
        *tables[:4],
    )
    correlation, warped = pl.pallas_call(
        compute_kernel,
        out_shape=[
            jax.ShapeDtypeStruct((PATCH_COLS, PATCH_SIZE, PATCH_SIZE), f32),
            jax.ShapeDtypeStruct((HEIGHT, WIDTH), f32),
        ],
        in_specs=[VMEM, ANY, ANY, VMEM, SMEM] + [ANY] * 8,
        out_specs=[ANY, ANY],
        scratch_shapes=space
        + [
            pltpu.VMEM((PATCH_SIZE, HALVES * LANES), bf16),
            pltpu.VMEM(parts_shape, bf16),
            pltpu.VMEM(parts_shape, f32),
            pltpu.VMEM(parts_shape, f32),
            pltpu.VMEM((PATCH_COLS, PATCH_SIZE, PATCH_SIZE), f32),
            pltpu.SemaphoreType.DMA((8,)),
            pltpu.SemaphoreType.DMA,
            pltpu.SemaphoreType.DMA((PATCH_COLS + 1,)),
        ],
        compiler_params=pltpu.CompilerParams(vmem_limit_bytes=VMEM_BYTES),
    )(other, parts, warped, scale, patch_mask[0], *tables)
    return correlation[None, None], warped[None]


def solution(mesh):
    placed = (
        P("gz", "gy", "gx"),
        P("gy", "gx", None),
        P("gz", "gy", "gx"),
        P("gz", "gy", "gx", None, None),
        P("gz", "gy", "gx", None),
        P("gz", "gy", "gx", None, None),
        P("gz", "gy", "gx", None, None),
    )
    tables = tuple(jnp.asarray(table) for table in make_tables())
    return jax.shard_map(
        functools.partial(body, tables),
        mesh=mesh,
        in_specs=placed,
        out_specs=(P("gz", "gy", "gx", None, None), P("gz", "gy", "gx")),
        check_vma=False,
    )
```

```python
import functools

import jax
import jax.numpy as jnp
import ml_dtypes
import numpy as np
from jax import lax
from jax.experimental import pallas as pl
from jax.experimental.pallas import tpu as pltpu
from jax.sharding import PartitionSpec as P

PATCH_SIZE = 160
STRIDE = 80
PATCH_COLS = 8
MARGIN = 24
DEST_SLOTS = 2
BLOCKS = 8
OWNERS = 16
PADDED = 128
SECTIONS = 32
HEIGHT = 80
WIDTH = 640
CHUNKS = 25
LANES = 128
HALO_ROWS = 48
STRIP_ROWS = HEIGHT + 2 * HALO_ROWS
STRIP_COLS = WIDTH + 2 * LANES
HALVES = 9
WAVES = 88
VMEM_BYTES = 60 * 2**20
FIXED = 24

epsilon = 1e-05
f32 = jnp.float32
bf16 = jnp.bfloat16
MESH = pl.DeviceIdType.MESH


def halves(table):
    high = table.astype(ml_dtypes.bfloat16)
    low = (table - high.astype(np.float64)).astype(ml_dtypes.bfloat16)
    return high, low


def make_tables():
    wave = np.arange(81)
    place = np.arange(PATCH_SIZE)
    angle = 2.0 * np.pi * (np.outer(wave, place) % PATCH_SIZE) / PATCH_SIZE
    cosine, sine = np.cos(angle), np.sin(angle)
    sine[0] = 0.0
    sine[80] = 0.0
    rows = np.zeros((2 * WAVES, PATCH_SIZE))
    rows[:81] = cosine
    rows[WAVES : WAVES + 81] = sine
    rows_high, rows_low = halves(rows)
    rows_both = np.concatenate([rows_high, rows_low], axis=0)
    row_sums = (rows_high.astype(np.float64) + rows_low.astype(np.float64)).sum(axis=1)
    row_sums = np.broadcast_to(row_sums[:, None], (2 * WAVES, LANES)).astype(np.float32)
    columns = np.zeros((LANES, 2 * LANES))
    columns[:STRIDE, :81] = cosine[:, :STRIDE].T
    columns[:STRIDE, LANES : LANES + 81] = sine[:, :STRIDE].T
    columns_high, columns_low = halves(columns)
    columns_twice = np.concatenate([columns_high, columns_high], axis=0)
    weight = np.ones(81)
    weight[0] = weight[80] = 0.5
    back_columns = np.zeros((2 * LANES, PATCH_SIZE))
    back_columns[:81] = weight[:, None] * cosine
    back_columns[LANES : LANES + 81] = weight[:, None] * sine
    back_columns = halves(back_columns)
    weight = np.full(81, 2.0)
    weight[0] = weight[80] = 1.0
    back_rows = np.zeros((PATCH_SIZE, 2 * WAVES))
    back_rows[:, :81] = (weight[:, None] * cosine).T
    back_rows[:, WAVES : WAVES + 81] = -(weight[:, None] * sine).T
    back_rows = halves(back_rows)
    return (rows_both, row_sums, columns_twice, columns_low, *back_columns, *back_rows)


def fill_table(owner_ref, cell_ref, count_ref, flow_ref, table_ref):
    owners, codes = [], []
    for block in range(BLOCKS):
        for entry in range(DEST_SLOTS):
            live = entry < count_ref[0, block]
            owners.append(jnp.where(live, owner_ref[entry, block], -1))
            codes.append(BLOCKS * block + cell_ref[entry, block])

    def one(owner, carry):
        first = second = jnp.int32(-1)
        for named, code in zip(owners, codes):
            match = named == owner
            second = jnp.where(match, first, second)
            first = jnp.where(match, code, first)
        for rank, code in enumerate((first, second)):
            block = jnp.maximum(code, 0) >> 3
            base = 8 * owner + 4 * rank
            table_ref[0, base] = block
            table_ref[0, base + 1] = jnp.where(code < 0, -1, code & 7)
            table_ref[0, base + 2] = flow_ref[0, block]
            table_ref[0, base + 3] = flow_ref[1, block]
        return carry

    lax.fori_loop(0, OWNERS, one, 0)


def chunk_of(index):
    line, place = index // 8, index % 8
    holds = ((place >= 1) & (place <= 6)) | (index == 0)
    return holds, jnp.where(index == 0, CHUNKS - 1, line * 6 + place - 1)


def holder_of(chunk):
    return jnp.where(chunk == CHUNKS - 1, 0, (chunk // 6) * 8 + chunk % 6 + 1)


def chunk_at(ref, chunk, row, column):
    rows = pl.ds(pl.multiple_of(row + 16 * (chunk // 5), 16), 16)
    columns = pl.ds(pl.multiple_of(column + LANES * (chunk % 5), LANES), LANES)
    return ref.at[rows, columns]


def exchange_kernel(
    tile_ref,
    partner_ref,
    owner_ref,
    cell_ref,
    count_ref,
    flow_ref,
    *rest,
):
    tables_hbm, (other_ref, parts_hbm, warped_hbm, scale_ref), rest = rest[:4], rest[4:8], rest[8:]
    tables_vmem, rest = rest[:4], rest[4:]
    (
        own_ref,
        slots_ref,
        info_ref,
        info_smem,
        held,
        sorted_,
        mirror,
        blocks,
        outgoing,
        tables,
        fixed,
        fixed_smem,
        table_smem,
        mirror_smem,
        strip,
        spectra,
        parts,
        cells,
        shifted,
        canvas,
        warped,
        send_sem,
        recv_sem,
        far_sem,
        slot_sem,
        local_sem,
        table_sem,
        out_sem,
    ) = rest
    gz, gy, gx = lax.axis_index("gz"), lax.axis_index("gy"), lax.axis_index("gx")
    half, core = gy // 2, gy % 2
    place = core * 4 + gx
    far_gy = 3 - gy
    near_gy = gy + 1 - 2 * core

    barrier = pltpu.get_barrier_semaphore()

    def greet(step, carry):
        pl.semaphore_signal(
            barrier, inc=1, device_id={"gz": lax.rem(gz + step, SECTIONS)}, device_id_type=MESH
        )
        return carry

    inner = (gy == 1) | (gy == 2)

    @pl.when(inner)
    def _():
        def greet_far(step, carry):
            section = lax.rem(gz + step, SECTIONS)
            pl.semaphore_signal(
                barrier, inc=1, device_id={"gz": section, "gy": far_gy}, device_id_type=MESH
            )
            return carry

        lax.fori_loop(1, SECTIONS, greet_far, 0)

    pl.semaphore_signal(barrier, inc=1, device_id={"gy": far_gy}, device_id_type=MESH)
    lax.fori_loop(1, SECTIONS, greet, 0)
    for step in range(1, 8):
        other_place = lax.rem(place + step, 8)
        pl.semaphore_signal(
            barrier,
            inc=1,
            device_id={"gy": 2 * half + other_place // 4, "gx": other_place % 4},
            device_id_type=MESH,
        )

    loads = [
        pltpu.make_async_copy(src, dst, table_sem.at[index])
        for index, (src, dst) in enumerate(zip(tables_hbm, tables_vmem))
    ]
    for load in loads:
        load.start()
    fixed[...] = jnp.round(flow_ref[...].astype(f32) * float(2**FIXED)).astype(jnp.int32)
    to_scalars = pltpu.make_async_copy(fixed, fixed_smem, local_sem)
    to_scalars.start()
    own_ref[pl.ds(HALO_ROWS, HEIGHT), pl.ds(LANES, WIDTH)] = tile_ref[...]
    top, bottom = pl.ds(0, HALO_ROWS), pl.ds(HALO_ROWS + HEIGHT, HALO_ROWS)
    left, right = pl.ds(0, LANES), pl.ds(LANES + WIDTH, LANES)
    middle = pl.ds(LANES, WIDTH)
    for ref in (own_ref, other_ref):

        @pl.when(gy == 0)
        def _():
            ref[top, middle] = jnp.zeros((HALO_ROWS, WIDTH), bf16)

        @pl.when(gy == 3)
        def _():
            ref[bottom, middle] = jnp.zeros((HALO_ROWS, WIDTH), bf16)

        @pl.when(gx == 0)
        def _():
            ref[:, left] = jnp.zeros((STRIP_ROWS, LANES), bf16)

        @pl.when(gx == 3)
        def _():
            ref[:, right] = jnp.zeros((STRIP_ROWS, LANES), bf16)

    lane = lax.broadcasted_iota(jnp.int32, (HEIGHT, LANES), 1)

    def cut_blocks(ref, base):
        for block in range(BLOCKS):
            start = STRIDE * block
            first = start // LANES * LANES
            shift = start - first
            width = LANES if shift + STRIDE <= LANES else 2 * LANES
            window = ref[:, first : first + width].astype(f32)
            if shift:
                window = pltpu.roll(window, width - shift, 1)[:, :LANES]
            blocks[base + block] = jnp.where(lane < STRIDE, window, 0.0).astype(bf16)

    def fill(kind, table):
        for target in range(8):
            base = 8 * (8 * half + target)
            for rank in range(2):
                block = table[0, base + 4 * rank]
                outgoing[kind, target, rank] = blocks[BLOCKS * kind + block]

    cut_blocks(tile_ref, 0)
    to_scalars.wait()
    fill_table(owner_ref, cell_ref, count_ref, fixed_smem, table_smem)
    to_vector = pltpu.make_async_copy(table_smem, tables.at[0], local_sem)
    to_vector.start()
    fill(0, table_smem)
    to_vector.wait()
    holds, mine = chunk_of(gz)
    @pl.when(inner)
    def _():
        pl.semaphore_wait(barrier, 2 * (SECTIONS - 1) + 8)

    @pl.when(jnp.logical_not(inner))
    def _():
        pl.semaphore_wait(barrier, SECTIONS - 1 + 8)

    def scatter(step, carry):
        chunk = lax.rem(mine + step, CHUNKS)
        holder = holder_of(chunk)

        @pl.when(holder != gz)
        def _():
            pltpu.make_async_remote_copy(
                src_ref=chunk_at(tile_ref, chunk, 0, 0),
                dst_ref=held.at[gz],
                send_sem=send_sem.at[0],
                recv_sem=recv_sem.at[0],
                device_id={"gz": holder},
                device_id_type=MESH,
            ).start()

        return carry

    def copy(src, dst, slot, device):
        return pltpu.make_async_remote_copy(
            src_ref=src,
            dst_ref=dst,
            send_sem=far_sem.at[0, slot],
            recv_sem=far_sem.at[1, slot],
            device_id=device,
            device_id_type=MESH,
        )

    near = {"gy": near_gy}
    own_down = copy(
        tile_ref.at[pl.ds(HEIGHT - HALO_ROWS, HALO_ROWS), :], own_ref.at[top, middle], 0, near
    )
    own_up = copy(tile_ref.at[pl.ds(0, HALO_ROWS), :], own_ref.at[bottom, middle], 0, near)
    to_far = copy(tile_ref, mirror, 1, {"gy": far_gy})
    table_far = copy(tables.at[0], tables.at[1], 2, {"gy": far_gy})

    def send_slots(kind):
        def one(step, carry):
            target = lax.rem(place + step, 8)
            device = {"gy": 2 * half + target // 4, "gx": target % 4}
            for src, dst, row in (
                (outgoing.at[kind, target], slots_ref.at[kind, place], 0),
                (tables.at[kind], info_ref.at[kind, place], 1),
            ):
                pltpu.make_async_remote_copy(
                    src_ref=src,
                    dst_ref=dst,
                    send_sem=slot_sem.at[0, kind, row],
                    recv_sem=slot_sem.at[1, kind, row],
                    device_id=device,
                    device_id_type=MESH,
                ).start()
            return carry

        lax.fori_loop(1, 8, one, 0)
        slots_ref[kind, place] = outgoing[kind, place]
        info_ref[kind, place] = tables[kind]

    lax.fori_loop(0, CHUNKS, scatter, 0)
    table_far.start()
    to_far.start()

    @pl.when(core == 0)
    def _():
        own_down.start()

    @pl.when(core == 1)
    def _():
        own_up.start()

    send_slots(0)

    first_row = jnp.where(gy == 1, 2, 0)
    rim_chunk = mine - 5 * first_row
    holds_rim = holds & inner & (rim_chunk >= 0) & (rim_chunk < 15)
    rim_chunk = jnp.where(holds_rim, rim_chunk, 0)
    rim_row = jnp.where(gy == 1, 0, HALO_ROWS + HEIGHT)

    @pl.when(holds)
    def _():
        held[gz] = chunk_at(tile_ref, mine, 0, 0)[...]
        pltpu.make_async_copy(
            held.at[pl.ds(0, SECTIONS - 1)], held.at[pl.ds(0, SECTIONS - 1)], recv_sem.at[0]
        ).wait()
        for section in range(SECTIONS):
            sorted_[section] = held[partner_ref[0, section]]

        def deliver(step, carry):
            section = lax.rem(gz + step, SECTIONS)
            pltpu.make_async_remote_copy(
                src_ref=sorted_.at[section],
                dst_ref=chunk_at(other_ref, mine, HALO_ROWS, LANES),
                send_sem=send_sem.at[1],
                recv_sem=recv_sem.at[1],
                device_id={"gz": section},
                device_id_type=MESH,
            ).start()
            return carry

        def deliver_far(step, carry):
            section = lax.rem(gz + step, SECTIONS)
            pltpu.make_async_remote_copy(
                src_ref=sorted_.at[section],
                dst_ref=chunk_at(other_ref, rim_chunk, rim_row, LANES),
                send_sem=send_sem.at[2],
                recv_sem=recv_sem.at[2],
                device_id={"gz": section, "gy": far_gy},
                device_id_type=MESH,
            ).start()
            return carry

        def send_far():
            lax.fori_loop(0, SECTIONS, deliver_far, 0)

        pl.when(holds_rim)(send_far)
        lax.fori_loop(1, SECTIONS, deliver, 0)
        chunk_at(other_ref, mine, HALO_ROWS, LANES)[...] = sorted_[gz]


    def side_copies(ref, slot):
        to_right = copy(
            ref.at[:, pl.ds(WIDTH, LANES)], ref.at[:, left], slot, {"gx": jnp.minimum(gx + 1, 3)}
        )
        to_left = copy(
            ref.at[:, pl.ds(LANES, LANES)], ref.at[:, right], slot + 1, {"gx": jnp.maximum(gx - 1, 0)}
        )
        return to_right, to_left

    def start_sides(copies):
        @pl.when(gx < 3)
        def _():
            copies[0].start()

        @pl.when(gx > 0)
        def _():
            copies[1].start()

    def receive_sides(copies):
        @pl.when(gx > 0)
        def _():
            copies[0].wait_recv()

        @pl.when(gx < 3)
        def _():
            copies[1].wait_recv()

    def sent_sides(copies):
        @pl.when(gx < 3)
        def _():
            copies[0].wait_send()

        @pl.when(gx > 0)
        def _():
            copies[1].wait_send()

    chunks = held.at[pl.ds(0, CHUNKS)]
    fewer = held.at[pl.ds(0, CHUNKS - 1)]
    near_from = pl.ds(pl.multiple_of(HEIGHT - (HEIGHT - HALO_ROWS) * core, 16), HALO_ROWS)
    near_to = pl.ds(pl.multiple_of((HALO_ROWS + HEIGHT) * core, 16), HALO_ROWS)
    rest_rows = pl.ds(pl.multiple_of(HALO_ROWS * core, 16), HALO_ROWS + HEIGHT)
    from_right, from_left = pl.ds(WIDTH, LANES), pl.ds(LANES, LANES)
    after, before = jnp.minimum(gx + 1, 3), jnp.maximum(gx - 1, 0)
    other_near = copy(
        other_ref.at[near_from, middle], other_ref.at[near_to, middle], 5, {"gy": near_gy}
    )
    other_right = [
        copy(other_ref.at[rest_rows, from_right], other_ref.at[rest_rows, left], 6, {"gx": after}),
        copy(
            other_ref.at[near_from, from_right],
            other_ref.at[near_to, left],
            7,
            {"gy": near_gy, "gx": after},
        ),
    ]
    other_left = [
        copy(other_ref.at[rest_rows, from_left], other_ref.at[rest_rows, right], 8, {"gx": before}),
        copy(
            other_ref.at[near_from, from_left],
            other_ref.at[near_to, right],
            9,
            {"gy": near_gy, "gx": before},
        ),
    ]
    own_sides = side_copies(own_ref, 3)

    def pass_rows():
        @pl.when(holds)
        def _():
            pltpu.make_async_copy(fewer, fewer, recv_sem.at[1]).wait()

        @pl.when(jnp.logical_not(holds))
        def _():
            pltpu.make_async_copy(chunks, chunks, recv_sem.at[1]).wait()

        @pl.when(inner)
        def _():
            rim = held.at[pl.ds(0, 15)]
            pltpu.make_async_copy(rim, rim, recv_sem.at[2]).wait()

        other_near.start()

        @pl.when(gx < 3)
        def _():
            for one in other_right:
                one.start()

        @pl.when(gx > 0)
        def _():
            for one in other_left:
                one.start()

    def receive_rims():
        other_near.wait_recv()

        @pl.when(gx > 0)
        def _():
            for one in other_right:
                one.wait_recv()

        @pl.when(gx < 3)
        def _():
            for one in other_left:
                one.wait_recv()

    def take_mirror():
        @pl.when(core == 1)
        def _():
            own_down.wait_recv()

        @pl.when(core == 0)
        def _():
            own_up.wait_recv()

        table_far.wait_recv()
        fetch = pltpu.make_async_copy(tables.at[1], mirror_smem, local_sem)
        fetch.start()
        to_far.wait_recv()

        @pl.when(gy == 1)
        def _():
            own_ref[bottom, middle] = mirror[pl.ds(0, HALO_ROWS), :]

        @pl.when(gy == 2)
        def _():
            own_ref[top, middle] = mirror[pl.ds(HEIGHT - HALO_ROWS, HALO_ROWS), :]

        start_sides(own_sides)
        cut_blocks(mirror, BLOCKS)
        fetch.wait()
        fill(1, mirror_smem)
        send_slots(1)

    stores = [
        pltpu.make_async_copy(parts, parts_hbm, out_sem.at[0]),
        pltpu.make_async_copy(warped, warped_hbm, out_sem.at[1]),
    ]

    def own_spectra():
        receive_sides(own_sides)
        for load in loads:
            load.wait()
        scales = forward(own_ref, strip, spectra, parts, *tables_vmem)
        stores[0].start()
        for patch, scale in enumerate(scales):
            scale_ref[patch : patch + 1, :] = jnp.broadcast_to(scale, (1, LANES))

    def warp():
        for kind in range(2):
            seven, seven_info = slots_ref.at[kind, pl.ds(0, 7)], info_ref.at[kind, pl.ds(0, 7)]
            pltpu.make_async_copy(seven, seven, slot_sem.at[1, kind, 0]).wait()
            pltpu.make_async_copy(seven_info, seven_info, slot_sem.at[1, kind, 1]).wait()
        fetch = pltpu.make_async_copy(info_ref, info_smem, local_sem)
        fetch.start()
        cells[...] = jnp.zeros_like(cells)
        shifted[...] = jnp.zeros_like(shifted)
        fetch.wait()
        add_up(slots_ref, info_smem, 8 * (4 * gy + gx), cells, shifted, canvas, warped)
        stores[1].start()

    take_mirror()
    own_spectra()
    pass_rows()
    warp()
    receive_rims()

    for kind in range(2):
        seven, seven_info = slots_ref.at[kind, pl.ds(0, 7)], info_ref.at[kind, pl.ds(0, 7)]
        pltpu.make_async_copy(seven, seven, slot_sem.at[0, kind, 0]).wait()
        pltpu.make_async_copy(seven_info, seven_info, slot_sem.at[0, kind, 1]).wait()

    @pl.when(holds)
    def _():
        pltpu.make_async_copy(fewer, fewer, send_sem.at[0]).wait()
        all_but_one = held.at[pl.ds(0, SECTIONS - 1)]
        pltpu.make_async_copy(all_but_one, all_but_one, send_sem.at[1]).wait()

    @pl.when(jnp.logical_not(holds))
    def _():
        pltpu.make_async_copy(chunks, chunks, send_sem.at[0]).wait()

    @pl.when(core == 0)
    def _():
        own_down.wait_send()

    @pl.when(core == 1)
    def _():
        own_up.wait_send()

    to_far.wait_send()
    table_far.wait_send()

    other_near.wait_send()

    @pl.when(gx < 3)
    def _():
        for one in other_right:
            one.wait_send()

    @pl.when(gx > 0)
    def _():
        for one in other_left:
            one.wait_send()

    @pl.when(holds_rim)
    def _():
        every = held.at[pl.ds(0, SECTIONS)]
        pltpu.make_async_copy(every, every, send_sem.at[2]).wait()

    sent_sides(own_sides)
    for store in stores:
        store.wait()


def split(value):
    high = value.astype(bf16)
    return high, (value - high.astype(f32)).astype(bf16)


def dot(left, right):
    return jnp.dot(left, right, preferred_element_type=f32)


def forward(ref, strip, spectra, parts, rows_both, row_sums, columns_twice, columns_low):
    lane = lax.broadcasted_iota(jnp.int32, (PATCH_SIZE, LANES), 1)
    means, squares = [], []
    for block in range(HALVES):
        start = LANES - 40 + STRIDE * block
        first = start // LANES * LANES
        shift = start - first
        width = LANES if shift + STRIDE <= LANES else 2 * LANES
        window = ref[8 : 8 + PATCH_SIZE, first : first + width].astype(f32)
        window = pltpu.roll(window, width - shift, 1)[:, :LANES]
        window = jnp.where(lane < STRIDE, window, 0.0)
        mean = jnp.sum(window, keepdims=True) * (1.0 / (PATCH_SIZE * STRIDE))
        centred = jnp.where(lane < STRIDE, window - mean, 0.0)
        means.append(mean)
        squares.append(jnp.sum(centred * centred, keepdims=True))
        strip[:, pl.ds(block * LANES, LANES)] = window.astype(bf16)

    level = sum(means) * (1.0 / HALVES) * row_sums[...]
    for block in range(HALVES):
        both = dot(rows_both[...], strip[:, pl.ds(block * LANES, LANES)])
        value = both[: 2 * WAVES] + both[2 * WAVES :] - level
        high, low = split(value)
        spectra[block, :, :LANES] = high
        spectra[block, :, LANES:] = low
    for block in range(HALVES):
        parts[block] = dot(spectra[block], columns_twice[...]) + dot(
            spectra[block, :, :LANES], columns_low[...]
        )

    count = PATCH_SIZE * STRIDE
    scales = []
    for patch in range(PATCH_COLS):
        gap = means[patch] - means[patch + 1]
        spread = (squares[patch] + squares[patch + 1] + gap * gap * (count / 2)) * (0.5 / count)
        scales.append(1.0 / jnp.sqrt(spread + epsilon))
    return scales


def add_up(slots_ref, info_smem, mine, cells, shifted, canvas, warped):
    unit = 1.0 / 2**FIXED

    def entries(source, carry):
        values, named = [], []
        for kind in range(2):
            for rank in range(2):
                base = mine + 4 * rank
                named.append(info_smem[kind, source, 0, base + 1])
                down = info_smem[kind, source, 0, base + 2]
                across = info_smem[kind, source, 0, base + 3]
                whole_down = jnp.clip(down >> FIXED, 1 - MARGIN, MARGIN - 1)
                whole_across = jnp.clip(across >> FIXED, 1 - MARGIN, MARGIN - 1)
                part_down = (down & (2**FIXED - 1)).astype(f32) * unit
                part_across = (across & (2**FIXED - 1)).astype(f32) * unit
                block = slots_ref[kind, source, rank].astype(f32)
                here = pltpu.roll(block, whole_across + MARGIN, 1)
                after = pltpu.roll(here, 1, 1)
                room = shifted.at[2 * kind + rank]
                room[pl.ds(MARGIN, HEIGHT), :] = here * (1.0 - part_across) + after * part_across
                here = room[pl.ds(MARGIN - whole_down, HEIGHT), :]
                after = room[pl.ds(MARGIN - 1 - whole_down, HEIGHT), :]
                value = here * (1.0 - part_down) + after * part_down
                values.append(value.astype(bf16).astype(f32))
        for cell in range(BLOCKS):
            total = cells[cell]
            for value, name in zip(values, named):
                total = total + value * (name == cell).astype(f32)
            cells[cell] = total
        return carry

    lax.fori_loop(0, 8, entries, 0)
    canvas[...] = jnp.zeros_like(canvas)
    for cell in range(BLOCKS):
        start = LANES - MARGIN + STRIDE * cell
        first = start // LANES * LANES
        shift = start - first
        wide = jnp.concatenate([cells[cell], jnp.zeros((HEIGHT, LANES), f32)], axis=1)
        if shift:
            wide = pltpu.roll(wide, shift, 1)
        canvas[:, first : first + 2 * LANES] = canvas[:, first : first + 2 * LANES] + wide
    warped[...] = canvas[:, LANES : LANES + WIDTH]


def compute_kernel(other_ref, parts_hbm, warped_in, scale_ref, mask_ref, *rest):
    tables_hbm, (correlation_hbm, warped_hbm), rest = rest[:8], rest[8:10], rest[10:]
    tables_vmem, rest = rest[:8], rest[8:]
    strip, spectra, own_parts, parts, result, table_sem, part_sem, out_sem = rest
    loads = [
        pltpu.make_async_copy(src, dst, table_sem.at[index])
        for index, (src, dst) in enumerate(zip(tables_hbm, tables_vmem))
    ]
    for load in loads:
        load.start()
    own_load = pltpu.make_async_copy(parts_hbm, own_parts, part_sem)
    own_load.start()
    stores = [pltpu.make_async_copy(warped_in, warped_hbm, out_sem.at[PATCH_COLS])]
    stores[0].start()
    back_columns_high, back_columns_low, back_rows_high, back_rows_low = tables_vmem[4:]
    for load in loads:
        load.wait()
    scales = forward(other_ref, strip, spectra, parts, *tables_vmem[:4])
    own_load.wait()

    row = lax.broadcasted_iota(jnp.int32, (WAVES, LANES), 0)
    column = lax.broadcasted_iota(jnp.int32, (WAVES, LANES), 1)
    constant = (row == 0) & (column == 0)
    odd = column % 2 == 1

    def spectrum(ref, first):
        def one(rows, lanes):
            later = ref[first + 1, rows, lanes]
            return ref[first, rows, lanes] + jnp.where(odd, -later, later)

        upper, lower = pl.ds(0, WAVES), pl.ds(WAVES, WAVES)
        low, high = pl.ds(0, LANES), pl.ds(LANES, LANES)
        a = jnp.where(constant, 0.0, one(upper, low))
        return a, one(lower, high), one(lower, low), one(upper, high)

    for patch in range(PATCH_COLS):
        scale = mask_ref[0, patch].astype(f32) * (2.0 / PATCH_SIZE**3)
        scale = scale * scales[patch] * scale_ref[patch : patch + 1, :]
        a, b, c, d = spectrum(own_parts, patch)
        e, f, g, h = spectrum(parts, patch)
        even_real = (a * e + b * f + c * g + d * h) * scale
        odd_real = (c * h + d * g - a * f - b * e) * scale
        even_imag = (c * e - d * f - a * g + b * h) * scale
        odd_imag = (d * e - c * f - a * h + b * g) * scale
        joined = jnp.concatenate(
            [
                jnp.concatenate([even_real, -odd_imag], axis=1),
                jnp.concatenate([even_imag, odd_real], axis=1),
            ],
            axis=0,
        )
        high, low = split(joined)
        half = (
            dot(high, back_columns_high[...])
            + dot(low, back_columns_high[...])
            + dot(high, back_columns_low[...])
        )
        high, low = split(half)
        result[patch] = (
            dot(back_rows_high[...], high)
            + dot(back_rows_high[...], low)
            + dot(back_rows_low[...], high)
        )
        stores.append(
            pltpu.make_async_copy(result.at[patch], correlation_hbm.at[patch], out_sem.at[patch])
        )
        stores[-1].start()
    for store in stores:
        store.wait()


VMEM = pl.BlockSpec(memory_space=pltpu.VMEM)
SMEM = pl.BlockSpec(memory_space=pltpu.SMEM)
ANY = pl.BlockSpec(memory_space=pl.ANY)


def body(tables, images, partner, patch_mask, flows, dest_count, dest_owner, dest_cell):
    space = [pltpu.VMEM(table.shape, table.dtype) for table in tables]
    parts_shape = (HALVES, 2 * WAVES, 2 * LANES)
    other, parts, warped, scale = pl.pallas_call(
        exchange_kernel,
        out_shape=[
            jax.ShapeDtypeStruct((STRIP_ROWS, STRIP_COLS), bf16),
            jax.ShapeDtypeStruct(parts_shape, f32),
            jax.ShapeDtypeStruct((HEIGHT, WIDTH), f32),
            jax.ShapeDtypeStruct((PATCH_COLS, LANES), f32),
        ],
        in_specs=[VMEM, SMEM, SMEM, SMEM, SMEM, VMEM] + [ANY] * 4,
        out_specs=[VMEM, ANY, ANY, VMEM],
        scratch_shapes=space[:4]
        + [
            pltpu.VMEM((STRIP_ROWS, STRIP_COLS), bf16),
            pltpu.VMEM((2, 8, 2, HEIGHT, LANES), bf16),
            pltpu.VMEM((2, 8, 1, 128), jnp.int32),
            pltpu.SMEM((2, 8, 1, 128), jnp.int32),
            pltpu.VMEM((SECTIONS, 16, LANES), bf16),
            pltpu.VMEM((SECTIONS, 16, LANES), bf16),
            pltpu.VMEM((HEIGHT, WIDTH), bf16),
            pltpu.VMEM((2 * BLOCKS, HEIGHT, LANES), bf16),
            pltpu.VMEM((2, 8, 2, HEIGHT, LANES), bf16),
            pltpu.VMEM((2, 1, 128), jnp.int32),
            pltpu.VMEM((2, BLOCKS), jnp.int32),
            pltpu.SMEM((2, BLOCKS), jnp.int32),
            pltpu.SMEM((1, 128), jnp.int32),
            pltpu.SMEM((1, 128), jnp.int32),
            pltpu.VMEM((PATCH_SIZE, HALVES * LANES), bf16),
            pltpu.VMEM(parts_shape, bf16),
            pltpu.VMEM(parts_shape, f32),
            pltpu.VMEM((BLOCKS, HEIGHT, LANES), f32),
            pltpu.VMEM((4, 128, LANES), f32),
            pltpu.VMEM((HEIGHT, STRIP_COLS), f32),
            pltpu.VMEM((HEIGHT, WIDTH), f32),
            pltpu.SemaphoreType.DMA((3,)),
            pltpu.SemaphoreType.DMA((3,)),
            pltpu.SemaphoreType.DMA((2, 10)),
            pltpu.SemaphoreType.DMA((2, 2, 2)),
            pltpu.SemaphoreType.DMA,
            pltpu.SemaphoreType.DMA((4,)),
            pltpu.SemaphoreType.DMA((2,)),
        ],
        compiler_params=pltpu.CompilerParams(
            collective_id=0, has_side_effects=True, vmem_limit_bytes=VMEM_BYTES
        ),
    )(
        images[0],
        partner[0],
        dest_owner[0, 0, 0].T,
        dest_cell[0, 0, 0].T,
        dest_count[0, 0],
        flows[0, 0, 0].T,
        *tables[:4],
    )
    correlation, warped = pl.pallas_call(
        compute_kernel,
        out_shape=[
            jax.ShapeDtypeStruct((PATCH_COLS, PATCH_SIZE, PATCH_SIZE), f32),
            jax.ShapeDtypeStruct((HEIGHT, WIDTH), f32),
        ],
        in_specs=[VMEM, ANY, ANY, VMEM, SMEM] + [ANY] * 8,
        out_specs=[ANY, ANY],
        scratch_shapes=space
        + [
            pltpu.VMEM((PATCH_SIZE, HALVES * LANES), bf16),
            pltpu.VMEM(parts_shape, bf16),
            pltpu.VMEM(parts_shape, f32),
            pltpu.VMEM(parts_shape, f32),
            pltpu.VMEM((PATCH_COLS, PATCH_SIZE, PATCH_SIZE), f32),
            pltpu.SemaphoreType.DMA((8,)),
            pltpu.SemaphoreType.DMA,
            pltpu.SemaphoreType.DMA((PATCH_COLS + 1,)),
        ],
        compiler_params=pltpu.CompilerParams(vmem_limit_bytes=VMEM_BYTES),
    )(other, parts, warped, scale, patch_mask[0], *tables)
    return correlation[None, None], warped[None]


def solution(mesh):
    placed = (
        P("gz", "gy", "gx"),
        P("gy", "gx", None),
        P("gz", "gy", "gx"),
        P("gz", "gy", "gx", None, None),
        P("gz", "gy", "gx", None),
        P("gz", "gy", "gx", None, None),
        P("gz", "gy", "gx", None, None),
    )
    tables = tuple(jnp.asarray(table) for table in make_tables())
    return jax.shard_map(
        functools.partial(body, tables),
        mesh=mesh,
        in_specs=placed,
        out_specs=(P("gz", "gy", "gx", None, None), P("gz", "gy", "gx")),
        check_vma=False,
    )
```

```python
import functools

import jax
import jax.numpy as jnp
import ml_dtypes
import numpy as np
from jax import lax
from jax.experimental import pallas as pl
from jax.experimental.pallas import tpu as pltpu
from jax.sharding import PartitionSpec as P

PATCH_SIZE = 160
STRIDE = 80
PATCH_COLS = 8
MARGIN = 24
DEST_SLOTS = 2
BLOCKS = 8
OWNERS = 16
PADDED = 128
SECTIONS = 32
HEIGHT = 80
WIDTH = 640
CHUNKS = 25
LANES = 128
HALO_ROWS = 48
STRIP_ROWS = HEIGHT + 2 * HALO_ROWS
STRIP_COLS = WIDTH + 2 * LANES
HALVES = 9
WAVES = 88
VMEM_BYTES = 60 * 2**20
FIXED = 24

epsilon = 1e-05
f32 = jnp.float32
bf16 = jnp.bfloat16
MESH = pl.DeviceIdType.MESH


def halves(table):
    high = table.astype(ml_dtypes.bfloat16)
    low = (table - high.astype(np.float64)).astype(ml_dtypes.bfloat16)
    return high, low


def make_tables():
    wave = np.arange(81)
    place = np.arange(PATCH_SIZE)
    angle = 2.0 * np.pi * (np.outer(wave, place) % PATCH_SIZE) / PATCH_SIZE
    cosine, sine = np.cos(angle), np.sin(angle)
    sine[0] = 0.0
    sine[80] = 0.0
    rows = np.zeros((2 * WAVES, PATCH_SIZE))
    rows[:81] = cosine
    rows[WAVES : WAVES + 81] = sine
    rows_high, rows_low = halves(rows)
    rows_both = np.concatenate([rows_high, rows_low], axis=0)
    row_sums = (rows_high.astype(np.float64) + rows_low.astype(np.float64)).sum(axis=1)
    row_sums = np.broadcast_to(row_sums[:, None], (2 * WAVES, LANES)).astype(np.float32)
    columns = np.zeros((LANES, 2 * LANES))
    columns[:STRIDE, :81] = cosine[:, :STRIDE].T
    columns[:STRIDE, LANES : LANES + 81] = sine[:, :STRIDE].T
    columns_high, columns_low = halves(columns)
    columns_twice = np.concatenate([columns_high, columns_high], axis=0)
    weight = np.ones(81)
    weight[0] = weight[80] = 0.5
    back_columns = np.zeros((2 * LANES, PATCH_SIZE))
    back_columns[:81] = weight[:, None] * cosine
    back_columns[LANES : LANES + 81] = weight[:, None] * sine
    back_columns = halves(back_columns)
    weight = np.full(81, 2.0)
    weight[0] = weight[80] = 1.0
    back_rows = np.zeros((PATCH_SIZE, 2 * WAVES))
    back_rows[:, :81] = (weight[:, None] * cosine).T
    back_rows[:, WAVES : WAVES + 81] = -(weight[:, None] * sine).T
    back_rows = halves(back_rows)
    return (rows_both, row_sums, columns_twice, columns_low, *back_columns, *back_rows)


def fill_table(owner_ref, cell_ref, count_ref, flow_ref, table_ref):
    owners, codes = [], []
    for block in range(BLOCKS):
        for entry in range(DEST_SLOTS):
            live = entry < count_ref[0, block]
            owners.append(jnp.where(live, owner_ref[entry, block], -1))
            codes.append(BLOCKS * block + cell_ref[entry, block])

    def one(owner, carry):
        first = second = jnp.int32(-1)
        for named, code in zip(owners, codes):
            match = named == owner
            second = jnp.where(match, first, second)
            first = jnp.where(match, code, first)
        for rank, code in enumerate((first, second)):
            block = jnp.maximum(code, 0) >> 3
            base = 8 * owner + 4 * rank
            table_ref[0, base] = block
            table_ref[0, base + 1] = jnp.where(code < 0, -1, code & 7)
            table_ref[0, base + 2] = flow_ref[0, block]
            table_ref[0, base + 3] = flow_ref[1, block]
        return carry

    lax.fori_loop(0, OWNERS, one, 0)


def chunk_of(index):
    line, place = index // 8, index % 8
    holds = ((place >= 1) & (place <= 6)) | (index == 0)
    return holds, jnp.where(index == 0, CHUNKS - 1, line * 6 + place - 1)


def holder_of(chunk):
    return jnp.where(chunk == CHUNKS - 1, 0, (chunk // 6) * 8 + chunk % 6 + 1)


def chunk_at(ref, chunk, row, column):
    rows = pl.ds(pl.multiple_of(row + 16 * (chunk // 5), 16), 16)
    columns = pl.ds(pl.multiple_of(column + LANES * (chunk % 5), LANES), LANES)
    return ref.at[rows, columns]


def exchange_kernel(
    tile_ref,
    partner_ref,
    owner_ref,
    cell_ref,
    count_ref,
    flow_ref,
    *rest,
):
    tables_hbm, (other_ref, parts_hbm, warped_hbm, scale_ref), rest = rest[:4], rest[4:8], rest[8:]
    tables_vmem, rest = rest[:4], rest[4:]
    (
        own_ref,
        slots_ref,
        info_ref,
        info_smem,
        held,
        sorted_,
        mirror,
        blocks,
        outgoing,
        tables,
        fixed,
        fixed_smem,
        table_smem,
        mirror_smem,
        strip,
        spectra,
        parts,
        cells,
        shifted,
        canvas,
        warped,
        send_sem,
        recv_sem,
        far_sem,
        slot_sem,
        local_sem,
        table_sem,
        out_sem,
    ) = rest
    gz, gy, gx = lax.axis_index("gz"), lax.axis_index("gy"), lax.axis_index("gx")
    half, core = gy // 2, gy % 2
    place = core * 4 + gx
    far_gy = 3 - gy
    near_gy = gy + 1 - 2 * core

    barrier = pltpu.get_barrier_semaphore()

    def greet(step, carry):
        pl.semaphore_signal(
            barrier, inc=1, device_id={"gz": lax.rem(gz + step, SECTIONS)}, device_id_type=MESH
        )
        return carry

    inner = (gy == 1) | (gy == 2)

    @pl.when(inner)
    def _():
        def greet_far(step, carry):
            section = lax.rem(gz + step, SECTIONS)
            pl.semaphore_signal(
                barrier, inc=1, device_id={"gz": section, "gy": far_gy}, device_id_type=MESH
            )
            return carry

        lax.fori_loop(1, SECTIONS, greet_far, 0)

    pl.semaphore_signal(barrier, inc=1, device_id={"gy": far_gy}, device_id_type=MESH)
    lax.fori_loop(1, SECTIONS, greet, 0)
    for step in range(1, 8):
        other_place = lax.rem(place + step, 8)
        pl.semaphore_signal(
            barrier,
            inc=1,
            device_id={"gy": 2 * half + other_place // 4, "gx": other_place % 4},
            device_id_type=MESH,
        )

    loads = [
        pltpu.make_async_copy(src, dst, table_sem.at[index])
        for index, (src, dst) in enumerate(zip(tables_hbm, tables_vmem))
    ]
    for load in loads:
        load.start()
    fixed[...] = jnp.round(flow_ref[...].astype(f32) * float(2**FIXED)).astype(jnp.int32)
    to_scalars = pltpu.make_async_copy(fixed, fixed_smem, local_sem)
    to_scalars.start()
    own_ref[pl.ds(HALO_ROWS, HEIGHT), pl.ds(LANES, WIDTH)] = tile_ref[...]
    top, bottom = pl.ds(0, HALO_ROWS), pl.ds(HALO_ROWS + HEIGHT, HALO_ROWS)
    left, right = pl.ds(0, LANES), pl.ds(LANES + WIDTH, LANES)
    middle = pl.ds(LANES, WIDTH)
    for ref in (own_ref, other_ref):

        @pl.when(gy == 0)
        def _():
            ref[top, middle] = jnp.zeros((HALO_ROWS, WIDTH), bf16)

        @pl.when(gy == 3)
        def _():
            ref[bottom, middle] = jnp.zeros((HALO_ROWS, WIDTH), bf16)

        @pl.when(gx == 0)
        def _():
            ref[:, left] = jnp.zeros((STRIP_ROWS, LANES), bf16)

        @pl.when(gx == 3)
        def _():
            ref[:, right] = jnp.zeros((STRIP_ROWS, LANES), bf16)

    lane = lax.broadcasted_iota(jnp.int32, (HEIGHT, LANES), 1)

    def cut_blocks(ref, base):
        for block in range(BLOCKS):
            start = STRIDE * block
            first = start // LANES * LANES
            shift = start - first
            width = LANES if shift + STRIDE <= LANES else 2 * LANES
            window = ref[:, first : first + width].astype(f32)
            if shift:
                window = pltpu.roll(window, width - shift, 1)[:, :LANES]
            blocks[base + block] = jnp.where(lane < STRIDE, window, 0.0).astype(bf16)

    def fill(kind, table):
        for target in range(8):
            base = 8 * (8 * half + target)
            for rank in range(2):
                block = table[0, base + 4 * rank]
                outgoing[kind, target, rank] = blocks[BLOCKS * kind + block]

    cut_blocks(tile_ref, 0)
    to_scalars.wait()
    fill_table(owner_ref, cell_ref, count_ref, fixed_smem, table_smem)
    to_vector = pltpu.make_async_copy(table_smem, tables.at[0], local_sem)
    to_vector.start()
    fill(0, table_smem)
    to_vector.wait()
    holds, mine = chunk_of(gz)
    @pl.when(inner)
    def _():
        pl.semaphore_wait(barrier, 2 * (SECTIONS - 1) + 8)

    @pl.when(jnp.logical_not(inner))
    def _():
        pl.semaphore_wait(barrier, SECTIONS - 1 + 8)

    line, upper = gz // 8, gz % 8 >= 4

    def far_section(step):
        to = jnp.where(upper, step // 4, 7 - step // 4)
        return 8 * lax.rem(line + 2 + step % 4, 4) + to

    def far_chunk(step):
        before = jnp.maximum(step - 1, 0)
        to = jnp.where(upper, before // 4, 5 - before // 4)
        return jnp.where(step == 0, CHUNKS - 1, 6 * lax.rem(line + 2 + before % 4, 4) + to)

    def scatter(step, carry):
        chunk = far_chunk(step)
        holder = holder_of(chunk)

        @pl.when(holder != gz)
        def _():
            pltpu.make_async_remote_copy(
                src_ref=chunk_at(tile_ref, chunk, 0, 0),
                dst_ref=held.at[gz],
                send_sem=send_sem.at[0],
                recv_sem=recv_sem.at[0],
                device_id={"gz": holder},
                device_id_type=MESH,
            ).start()

        return carry

    def copy(src, dst, slot, device):
        return pltpu.make_async_remote_copy(
            src_ref=src,
            dst_ref=dst,
            send_sem=far_sem.at[0, slot],
            recv_sem=far_sem.at[1, slot],
            device_id=device,
            device_id_type=MESH,
        )

    near = {"gy": near_gy}
    own_down = copy(
        tile_ref.at[pl.ds(HEIGHT - HALO_ROWS, HALO_ROWS), :], own_ref.at[top, middle], 0, near
    )
    own_up = copy(tile_ref.at[pl.ds(0, HALO_ROWS), :], own_ref.at[bottom, middle], 0, near)
    to_far = copy(tile_ref, mirror, 1, {"gy": far_gy})
    table_far = copy(tables.at[0], tables.at[1], 2, {"gy": far_gy})

    def send_slots(kind):
        def one(step, carry):
            target = lax.rem(place + step, 8)
            device = {"gy": 2 * half + target // 4, "gx": target % 4}
            for src, dst, row in (
                (outgoing.at[kind, target], slots_ref.at[kind, place], 0),
                (tables.at[kind], info_ref.at[kind, place], 1),
            ):
                pltpu.make_async_remote_copy(
                    src_ref=src,
                    dst_ref=dst,
                    send_sem=slot_sem.at[0, kind, row],
                    recv_sem=slot_sem.at[1, kind, row],
                    device_id=device,
                    device_id_type=MESH,
                ).start()
            return carry

        lax.fori_loop(1, 8, one, 0)
        slots_ref[kind, place] = outgoing[kind, place]
        info_ref[kind, place] = tables[kind]

    lax.fori_loop(0, CHUNKS, scatter, 0)
    table_far.start()
    to_far.start()

    @pl.when(core == 0)
    def _():
        own_down.start()

    @pl.when(core == 1)
    def _():
        own_up.start()

    send_slots(0)

    first_row = jnp.where(gy == 1, 2, 0)
    rim_chunk = mine - 5 * first_row
    holds_rim = holds & inner & (rim_chunk >= 0) & (rim_chunk < 15)
    rim_chunk = jnp.where(holds_rim, rim_chunk, 0)
    rim_row = jnp.where(gy == 1, 0, HALO_ROWS + HEIGHT)

    @pl.when(holds)
    def _():
        held[gz] = chunk_at(tile_ref, mine, 0, 0)[...]
        pltpu.make_async_copy(
            held.at[pl.ds(0, SECTIONS - 1)], held.at[pl.ds(0, SECTIONS - 1)], recv_sem.at[0]
        ).wait()
        for section in range(SECTIONS):
            sorted_[section] = held[partner_ref[0, section]]

        def deliver(step, carry):
            section = far_section(step)

            @pl.when(section != gz)
            def _():
                pltpu.make_async_remote_copy(
                    src_ref=sorted_.at[section],
                    dst_ref=chunk_at(other_ref, mine, HALO_ROWS, LANES),
                    send_sem=send_sem.at[1],
                    recv_sem=recv_sem.at[1],
                    device_id={"gz": section},
                    device_id_type=MESH,
                ).start()

            return carry

        def deliver_far(step, carry):
            section = lax.rem(gz + step, SECTIONS)
            pltpu.make_async_remote_copy(
                src_ref=sorted_.at[section],
                dst_ref=chunk_at(other_ref, rim_chunk, rim_row, LANES),
                send_sem=send_sem.at[2],
                recv_sem=recv_sem.at[2],
                device_id={"gz": section, "gy": far_gy},
                device_id_type=MESH,
            ).start()
            return carry

        def send_far():
            lax.fori_loop(0, SECTIONS, deliver_far, 0)

        pl.when(holds_rim)(send_far)
        lax.fori_loop(0, SECTIONS, deliver, 0)
        chunk_at(other_ref, mine, HALO_ROWS, LANES)[...] = sorted_[gz]


    def side_copies(ref, slot):
        to_right = copy(
            ref.at[:, pl.ds(WIDTH, LANES)], ref.at[:, left], slot, {"gx": jnp.minimum(gx + 1, 3)}
        )
        to_left = copy(
            ref.at[:, pl.ds(LANES, LANES)], ref.at[:, right], slot + 1, {"gx": jnp.maximum(gx - 1, 0)}
        )
        return to_right, to_left

    def start_sides(copies):
        @pl.when(gx < 3)
        def _():
            copies[0].start()

        @pl.when(gx > 0)
        def _():
            copies[1].start()

    def receive_sides(copies):
        @pl.when(gx > 0)
        def _():
            copies[0].wait_recv()

        @pl.when(gx < 3)
        def _():
            copies[1].wait_recv()

    def sent_sides(copies):
        @pl.when(gx < 3)
        def _():
            copies[0].wait_send()

        @pl.when(gx > 0)
        def _():
            copies[1].wait_send()

    chunks = held.at[pl.ds(0, CHUNKS)]
    fewer = held.at[pl.ds(0, CHUNKS - 1)]
    near_from = pl.ds(pl.multiple_of(HEIGHT - (HEIGHT - HALO_ROWS) * core, 16), HALO_ROWS)
    near_to = pl.ds(pl.multiple_of((HALO_ROWS + HEIGHT) * core, 16), HALO_ROWS)
    rest_rows = pl.ds(pl.multiple_of(HALO_ROWS * core, 16), HALO_ROWS + HEIGHT)
    from_right, from_left = pl.ds(WIDTH, LANES), pl.ds(LANES, LANES)
    after, before = jnp.minimum(gx + 1, 3), jnp.maximum(gx - 1, 0)
    other_near = copy(
        other_ref.at[near_from, middle], other_ref.at[near_to, middle], 5, {"gy": near_gy}
    )
    other_right = [
        copy(other_ref.at[rest_rows, from_right], other_ref.at[rest_rows, left], 6, {"gx": after}),
        copy(
            other_ref.at[near_from, from_right],
            other_ref.at[near_to, left],
            7,
            {"gy": near_gy, "gx": after},
        ),
    ]
    other_left = [
        copy(other_ref.at[rest_rows, from_left], other_ref.at[rest_rows, right], 8, {"gx": before}),
        copy(
            other_ref.at[near_from, from_left],
            other_ref.at[near_to, right],
            9,
            {"gy": near_gy, "gx": before},
        ),
    ]
    own_sides = side_copies(own_ref, 3)

    def pass_rows():
        @pl.when(holds)
        def _():
            pltpu.make_async_copy(fewer, fewer, recv_sem.at[1]).wait()

        @pl.when(jnp.logical_not(holds))
        def _():
            pltpu.make_async_copy(chunks, chunks, recv_sem.at[1]).wait()

        @pl.when(inner)
        def _():
            rim = held.at[pl.ds(0, 15)]
            pltpu.make_async_copy(rim, rim, recv_sem.at[2]).wait()

        other_near.start()

        @pl.when(gx < 3)
        def _():
            for one in other_right:
                one.start()

        @pl.when(gx > 0)
        def _():
            for one in other_left:
                one.start()

    def receive_rims():
        other_near.wait_recv()

        @pl.when(gx > 0)
        def _():
            for one in other_right:
                one.wait_recv()

        @pl.when(gx < 3)
        def _():
            for one in other_left:
                one.wait_recv()

    def take_mirror():
        @pl.when(core == 1)
        def _():
            own_down.wait_recv()

        @pl.when(core == 0)
        def _():
            own_up.wait_recv()

        table_far.wait_recv()
        fetch = pltpu.make_async_copy(tables.at[1], mirror_smem, local_sem)
        fetch.start()
        to_far.wait_recv()

        @pl.when(gy == 1)
        def _():
            own_ref[bottom, middle] = mirror[pl.ds(0, HALO_ROWS), :]

        @pl.when(gy == 2)
        def _():
            own_ref[top, middle] = mirror[pl.ds(HEIGHT - HALO_ROWS, HALO_ROWS), :]

        start_sides(own_sides)
        cut_blocks(mirror, BLOCKS)
        fetch.wait()
        fill(1, mirror_smem)
        send_slots(1)

    stores = [
        pltpu.make_async_copy(parts, parts_hbm, out_sem.at[0]),
        pltpu.make_async_copy(warped, warped_hbm, out_sem.at[1]),
    ]

    def own_spectra():
        receive_sides(own_sides)
        for load in loads:
            load.wait()
        scales = forward(own_ref, strip, spectra, parts, *tables_vmem)
        stores[0].start()
        for patch, scale in enumerate(scales):
            scale_ref[patch : patch + 1, :] = jnp.broadcast_to(scale, (1, LANES))

    def warp():
        for kind in range(2):
            seven, seven_info = slots_ref.at[kind, pl.ds(0, 7)], info_ref.at[kind, pl.ds(0, 7)]
            pltpu.make_async_copy(seven, seven, slot_sem.at[1, kind, 0]).wait()
            pltpu.make_async_copy(seven_info, seven_info, slot_sem.at[1, kind, 1]).wait()
        fetch = pltpu.make_async_copy(info_ref, info_smem, local_sem)
        fetch.start()
        cells[...] = jnp.zeros_like(cells)
        shifted[...] = jnp.zeros_like(shifted)
        fetch.wait()
        add_up(slots_ref, info_smem, 8 * (4 * gy + gx), cells, shifted, canvas, warped)
        stores[1].start()

    take_mirror()
    own_spectra()
    pass_rows()
    warp()
    receive_rims()

    for kind in range(2):
        seven, seven_info = slots_ref.at[kind, pl.ds(0, 7)], info_ref.at[kind, pl.ds(0, 7)]
        pltpu.make_async_copy(seven, seven, slot_sem.at[0, kind, 0]).wait()
        pltpu.make_async_copy(seven_info, seven_info, slot_sem.at[0, kind, 1]).wait()

    @pl.when(holds)
    def _():
        pltpu.make_async_copy(fewer, fewer, send_sem.at[0]).wait()
        all_but_one = held.at[pl.ds(0, SECTIONS - 1)]
        pltpu.make_async_copy(all_but_one, all_but_one, send_sem.at[1]).wait()

    @pl.when(jnp.logical_not(holds))
    def _():
        pltpu.make_async_copy(chunks, chunks, send_sem.at[0]).wait()

    @pl.when(core == 0)
    def _():
        own_down.wait_send()

    @pl.when(core == 1)
    def _():
        own_up.wait_send()

    to_far.wait_send()
    table_far.wait_send()

    other_near.wait_send()

    @pl.when(gx < 3)
    def _():
        for one in other_right:
            one.wait_send()

    @pl.when(gx > 0)
    def _():
        for one in other_left:
            one.wait_send()

    @pl.when(holds_rim)
    def _():
        every = held.at[pl.ds(0, SECTIONS)]
        pltpu.make_async_copy(every, every, send_sem.at[2]).wait()

    sent_sides(own_sides)
    for store in stores:
        store.wait()


def split(value):
    high = value.astype(bf16)
    return high, (value - high.astype(f32)).astype(bf16)


def dot(left, right):
    return jnp.dot(left, right, preferred_element_type=f32)


def forward(ref, strip, spectra, parts, rows_both, row_sums, columns_twice, columns_low):
    lane = lax.broadcasted_iota(jnp.int32, (PATCH_SIZE, LANES), 1)
    means, squares = [], []
    for block in range(HALVES):
        start = LANES - 40 + STRIDE * block
        first = start // LANES * LANES
        shift = start - first
        width = LANES if shift + STRIDE <= LANES else 2 * LANES
        window = ref[8 : 8 + PATCH_SIZE, first : first + width].astype(f32)
        window = pltpu.roll(window, width - shift, 1)[:, :LANES]
        window = jnp.where(lane < STRIDE, window, 0.0)
        mean = jnp.sum(window, keepdims=True) * (1.0 / (PATCH_SIZE * STRIDE))
        centred = jnp.where(lane < STRIDE, window - mean, 0.0)
        means.append(mean)
        squares.append(jnp.sum(centred * centred, keepdims=True))
        strip[:, pl.ds(block * LANES, LANES)] = window.astype(bf16)

    level = sum(means) * (1.0 / HALVES) * row_sums[...]
    for block in range(HALVES):
        both = dot(rows_both[...], strip[:, pl.ds(block * LANES, LANES)])
        value = both[: 2 * WAVES] + both[2 * WAVES :] - level
        high, low = split(value)
        spectra[block, :, :LANES] = high
        spectra[block, :, LANES:] = low
    for block in range(HALVES):
        parts[block] = dot(spectra[block], columns_twice[...]) + dot(
            spectra[block, :, :LANES], columns_low[...]
        )

    count = PATCH_SIZE * STRIDE
    scales = []
    for patch in range(PATCH_COLS):
        gap = means[patch] - means[patch + 1]
        spread = (squares[patch] + squares[patch + 1] + gap * gap * (count / 2)) * (0.5 / count)
        scales.append(1.0 / jnp.sqrt(spread + epsilon))
    return scales


def add_up(slots_ref, info_smem, mine, cells, shifted, canvas, warped):
    unit = 1.0 / 2**FIXED

    def entries(source, carry):
        values, named = [], []
        for kind in range(2):
            for rank in range(2):
                base = mine + 4 * rank
                named.append(info_smem[kind, source, 0, base + 1])
                down = info_smem[kind, source, 0, base + 2]
                across = info_smem[kind, source, 0, base + 3]
                whole_down = jnp.clip(down >> FIXED, 1 - MARGIN, MARGIN - 1)
                whole_across = jnp.clip(across >> FIXED, 1 - MARGIN, MARGIN - 1)
                part_down = (down & (2**FIXED - 1)).astype(f32) * unit
                part_across = (across & (2**FIXED - 1)).astype(f32) * unit
                block = slots_ref[kind, source, rank].astype(f32)
                here = pltpu.roll(block, whole_across + MARGIN, 1)
                after = pltpu.roll(here, 1, 1)
                room = shifted.at[2 * kind + rank]
                room[pl.ds(MARGIN, HEIGHT), :] = here * (1.0 - part_across) + after * part_across
                here = room[pl.ds(MARGIN - whole_down, HEIGHT), :]
                after = room[pl.ds(MARGIN - 1 - whole_down, HEIGHT), :]
                value = here * (1.0 - part_down) + after * part_down
                values.append(value.astype(bf16).astype(f32))
        for cell in range(BLOCKS):
            total = cells[cell]
            for value, name in zip(values, named):
                total = total + value * (name == cell).astype(f32)
            cells[cell] = total
        return carry

    lax.fori_loop(0, 8, entries, 0)
    canvas[...] = jnp.zeros_like(canvas)
    for cell in range(BLOCKS):
        start = LANES - MARGIN + STRIDE * cell
        first = start // LANES * LANES
        shift = start - first
        wide = jnp.concatenate([cells[cell], jnp.zeros((HEIGHT, LANES), f32)], axis=1)
        if shift:
            wide = pltpu.roll(wide, shift, 1)
        canvas[:, first : first + 2 * LANES] = canvas[:, first : first + 2 * LANES] + wide
    warped[...] = canvas[:, LANES : LANES + WIDTH]


def compute_kernel(other_ref, parts_hbm, warped_in, scale_ref, mask_ref, *rest):
    tables_hbm, (correlation_hbm, warped_hbm), rest = rest[:8], rest[8:10], rest[10:]
    tables_vmem, rest = rest[:8], rest[8:]
    strip, spectra, own_parts, parts, result, table_sem, part_sem, out_sem = rest
    loads = [
        pltpu.make_async_copy(src, dst, table_sem.at[index])
        for index, (src, dst) in enumerate(zip(tables_hbm, tables_vmem))
    ]
    for load in loads:
        load.start()
    own_load = pltpu.make_async_copy(parts_hbm, own_parts, part_sem)
    own_load.start()
    stores = [pltpu.make_async_copy(warped_in, warped_hbm, out_sem.at[PATCH_COLS])]
    stores[0].start()
    back_columns_high, back_columns_low, back_rows_high, back_rows_low = tables_vmem[4:]
    for load in loads:
        load.wait()
    scales = forward(other_ref, strip, spectra, parts, *tables_vmem[:4])
    own_load.wait()

    row = lax.broadcasted_iota(jnp.int32, (WAVES, LANES), 0)
    column = lax.broadcasted_iota(jnp.int32, (WAVES, LANES), 1)
    constant = (row == 0) & (column == 0)
    odd = column % 2 == 1

    def spectrum(ref, first):
        def one(rows, lanes):
            later = ref[first + 1, rows, lanes]
            return ref[first, rows, lanes] + jnp.where(odd, -later, later)

        upper, lower = pl.ds(0, WAVES), pl.ds(WAVES, WAVES)
        low, high = pl.ds(0, LANES), pl.ds(LANES, LANES)
        a = jnp.where(constant, 0.0, one(upper, low))
        return a, one(lower, high), one(lower, low), one(upper, high)

    for patch in range(PATCH_COLS):
        scale = mask_ref[0, patch].astype(f32) * (2.0 / PATCH_SIZE**3)
        scale = scale * scales[patch] * scale_ref[patch : patch + 1, :]
        a, b, c, d = spectrum(own_parts, patch)
        e, f, g, h = spectrum(parts, patch)
        even_real = (a * e + b * f + c * g + d * h) * scale
        odd_real = (c * h + d * g - a * f - b * e) * scale
        even_imag = (c * e - d * f - a * g + b * h) * scale
        odd_imag = (d * e - c * f - a * h + b * g) * scale
        joined = jnp.concatenate(
            [
                jnp.concatenate([even_real, -odd_imag], axis=1),
                jnp.concatenate([even_imag, odd_real], axis=1),
            ],
            axis=0,
        )
        high, low = split(joined)
        half = (
            dot(high, back_columns_high[...])
            + dot(low, back_columns_high[...])
            + dot(high, back_columns_low[...])
        )
        high, low = split(half)
        result[patch] = (
            dot(back_rows_high[...], high)
            + dot(back_rows_high[...], low)
            + dot(back_rows_low[...], high)
        )
        stores.append(
            pltpu.make_async_copy(result.at[patch], correlation_hbm.at[patch], out_sem.at[patch])
        )
        stores[-1].start()
    for store in stores:
        store.wait()


VMEM = pl.BlockSpec(memory_space=pltpu.VMEM)
SMEM = pl.BlockSpec(memory_space=pltpu.SMEM)
ANY = pl.BlockSpec(memory_space=pl.ANY)


def body(tables, images, partner, patch_mask, flows, dest_count, dest_owner, dest_cell):
    space = [pltpu.VMEM(table.shape, table.dtype) for table in tables]
    parts_shape = (HALVES, 2 * WAVES, 2 * LANES)
    other, parts, warped, scale = pl.pallas_call(
        exchange_kernel,
        out_shape=[
            jax.ShapeDtypeStruct((STRIP_ROWS, STRIP_COLS), bf16),
            jax.ShapeDtypeStruct(parts_shape, f32),
            jax.ShapeDtypeStruct((HEIGHT, WIDTH), f32),
            jax.ShapeDtypeStruct((PATCH_COLS, LANES), f32),
        ],
        in_specs=[VMEM, SMEM, SMEM, SMEM, SMEM, VMEM] + [ANY] * 4,
        out_specs=[VMEM, ANY, ANY, VMEM],
        scratch_shapes=space[:4]
        + [
            pltpu.VMEM((STRIP_ROWS, STRIP_COLS), bf16),
            pltpu.VMEM((2, 8, 2, HEIGHT, LANES), bf16),
            pltpu.VMEM((2, 8, 1, 128), jnp.int32),
            pltpu.SMEM((2, 8, 1, 128), jnp.int32),
            pltpu.VMEM((SECTIONS, 16, LANES), bf16),
            pltpu.VMEM((SECTIONS, 16, LANES), bf16),
            pltpu.VMEM((HEIGHT, WIDTH), bf16),
            pltpu.VMEM((2 * BLOCKS, HEIGHT, LANES), bf16),
            pltpu.VMEM((2, 8, 2, HEIGHT, LANES), bf16),
            pltpu.VMEM((2, 1, 128), jnp.int32),
            pltpu.VMEM((2, BLOCKS), jnp.int32),
            pltpu.SMEM((2, BLOCKS), jnp.int32),
            pltpu.SMEM((1, 128), jnp.int32),
            pltpu.SMEM((1, 128), jnp.int32),
            pltpu.VMEM((PATCH_SIZE, HALVES * LANES), bf16),
            pltpu.VMEM(parts_shape, bf16),
            pltpu.VMEM(parts_shape, f32),
            pltpu.VMEM((BLOCKS, HEIGHT, LANES), f32),
            pltpu.VMEM((4, 128, LANES), f32),
            pltpu.VMEM((HEIGHT, STRIP_COLS), f32),
            pltpu.VMEM((HEIGHT, WIDTH), f32),
            pltpu.SemaphoreType.DMA((3,)),
            pltpu.SemaphoreType.DMA((3,)),
            pltpu.SemaphoreType.DMA((2, 10)),
            pltpu.SemaphoreType.DMA((2, 2, 2)),
            pltpu.SemaphoreType.DMA,
            pltpu.SemaphoreType.DMA((4,)),
            pltpu.SemaphoreType.DMA((2,)),
        ],
        compiler_params=pltpu.CompilerParams(
            collective_id=0, has_side_effects=True, vmem_limit_bytes=VMEM_BYTES
        ),
    )(
        images[0],
        partner[0],
        dest_owner[0, 0, 0].T,
        dest_cell[0, 0, 0].T,
        dest_count[0, 0],
        flows[0, 0, 0].T,
        *tables[:4],
    )
    correlation, warped = pl.pallas_call(
        compute_kernel,
        out_shape=[
            jax.ShapeDtypeStruct((PATCH_COLS, PATCH_SIZE, PATCH_SIZE), f32),
            jax.ShapeDtypeStruct((HEIGHT, WIDTH), f32),
        ],
        in_specs=[VMEM, ANY, ANY, VMEM, SMEM] + [ANY] * 8,
        out_specs=[ANY, ANY],
        scratch_shapes=space
        + [
            pltpu.VMEM((PATCH_SIZE, HALVES * LANES), bf16),
            pltpu.VMEM(parts_shape, bf16),
            pltpu.VMEM(parts_shape, f32),
            pltpu.VMEM(parts_shape, f32),
            pltpu.VMEM((PATCH_COLS, PATCH_SIZE, PATCH_SIZE), f32),
            pltpu.SemaphoreType.DMA((8,)),
            pltpu.SemaphoreType.DMA,
            pltpu.SemaphoreType.DMA((PATCH_COLS + 1,)),
        ],
        compiler_params=pltpu.CompilerParams(vmem_limit_bytes=VMEM_BYTES),
    )(other, parts, warped, scale, patch_mask[0], *tables)
    return correlation[None, None], warped[None]


def solution(mesh):
    placed = (
        P("gz", "gy", "gx"),
        P("gy", "gx", None),
        P("gz", "gy", "gx"),
        P("gz", "gy", "gx", None, None),
        P("gz", "gy", "gx", None),
        P("gz", "gy", "gx", None, None),
        P("gz", "gy", "gx", None, None),
    )
    tables = tuple(jnp.asarray(table) for table in make_tables())
    return jax.shard_map(
        functools.partial(body, tables),
        mesh=mesh,
        in_specs=placed,
        out_specs=(P("gz", "gy", "gx", None, None), P("gz", "gy", "gx")),
        check_vma=False,
    )
```

```python
import functools

import jax
import jax.numpy as jnp
import ml_dtypes
import numpy as np
from jax import lax
from jax.experimental import pallas as pl
from jax.experimental.pallas import tpu as pltpu
from jax.sharding import PartitionSpec as P

PATCH_SIZE = 160
STRIDE = 80
PATCH_COLS = 8
MARGIN = 24
DEST_SLOTS = 2
BLOCKS = 8
OWNERS = 16
PADDED = 128
SECTIONS = 32
HEIGHT = 80
WIDTH = 640
CHUNKS = 25
LANES = 128
HALO_ROWS = 48
STRIP_ROWS = HEIGHT + 2 * HALO_ROWS
STRIP_COLS = WIDTH + 2 * LANES
HALVES = 9
WAVES = 88
VMEM_BYTES = 60 * 2**20
FIXED = 24

epsilon = 1e-05
f32 = jnp.float32
bf16 = jnp.bfloat16
MESH = pl.DeviceIdType.MESH


def halves(table):
    high = table.astype(ml_dtypes.bfloat16)
    low = (table - high.astype(np.float64)).astype(ml_dtypes.bfloat16)
    return high, low


def make_tables():
    wave = np.arange(81)
    place = np.arange(PATCH_SIZE)
    angle = 2.0 * np.pi * (np.outer(wave, place) % PATCH_SIZE) / PATCH_SIZE
    cosine, sine = np.cos(angle), np.sin(angle)
    sine[0] = 0.0
    sine[80] = 0.0
    rows = np.zeros((2 * WAVES, PATCH_SIZE))
    rows[:81] = cosine
    rows[WAVES : WAVES + 81] = sine
    rows_high, rows_low = halves(rows)
    rows_both = np.concatenate([rows_high, rows_low], axis=0)
    row_sums = (rows_high.astype(np.float64) + rows_low.astype(np.float64)).sum(axis=1)
    row_sums = np.broadcast_to(row_sums[:, None], (2 * WAVES, LANES)).astype(np.float32)
    columns = np.zeros((LANES, 2 * LANES))
    columns[:STRIDE, :81] = cosine[:, :STRIDE].T
    columns[:STRIDE, LANES : LANES + 81] = sine[:, :STRIDE].T
    columns_high, columns_low = halves(columns)
    columns_twice = np.concatenate([columns_high, columns_high], axis=0)
    weight = np.ones(81)
    weight[0] = weight[80] = 0.5
    back_columns = np.zeros((2 * LANES, PATCH_SIZE))
    back_columns[:81] = weight[:, None] * cosine
    back_columns[LANES : LANES + 81] = weight[:, None] * sine
    back_columns = halves(back_columns)
    weight = np.full(81, 2.0)
    weight[0] = weight[80] = 1.0
    back_rows = np.zeros((PATCH_SIZE, 2 * WAVES))
    back_rows[:, :81] = (weight[:, None] * cosine).T
    back_rows[:, WAVES : WAVES + 81] = -(weight[:, None] * sine).T
    back_rows = np.concatenate(halves(back_rows), axis=0)
    return (rows_both, row_sums, columns_twice, columns_low, *back_columns, back_rows)


def fill_table(owner_ref, cell_ref, count_ref, flow_ref, table_ref):
    owners, codes = [], []
    for block in range(BLOCKS):
        for entry in range(DEST_SLOTS):
            live = entry < count_ref[0, block]
            owners.append(jnp.where(live, owner_ref[entry, block], -1))
            codes.append(BLOCKS * block + cell_ref[entry, block])

    def one(owner, carry):
        first = second = jnp.int32(-1)
        for named, code in zip(owners, codes):
            match = named == owner
            second = jnp.where(match, first, second)
            first = jnp.where(match, code, first)
        for rank, code in enumerate((first, second)):
            block = jnp.maximum(code, 0) >> 3
            base = 8 * owner + 4 * rank
            table_ref[0, base] = block
            table_ref[0, base + 1] = jnp.where(code < 0, -1, code & 7)
            table_ref[0, base + 2] = flow_ref[0, block]
            table_ref[0, base + 3] = flow_ref[1, block]
        return carry

    lax.fori_loop(0, OWNERS, one, 0)


def chunk_of(index):
    line, place = index // 8, index % 8
    holds = ((place >= 1) & (place <= 6)) | (index == 0)
    return holds, jnp.where(index == 0, CHUNKS - 1, line * 6 + place - 1)


def holder_of(chunk):
    return jnp.where(chunk == CHUNKS - 1, 0, (chunk // 6) * 8 + chunk % 6 + 1)


def chunk_at(ref, chunk, row, column):
    rows = pl.ds(pl.multiple_of(row + 16 * (chunk // 5), 16), 16)
    columns = pl.ds(pl.multiple_of(column + LANES * (chunk % 5), LANES), LANES)
    return ref.at[rows, columns]


def exchange_kernel(
    tile_ref,
    partner_ref,
    owner_ref,
    cell_ref,
    count_ref,
    flow_ref,
    *rest,
):
    tables_hbm, (other_ref, parts_hbm, warped_hbm, scale_ref), rest = rest[:4], rest[4:8], rest[8:]
    tables_vmem, rest = rest[:4], rest[4:]
    (
        own_ref,
        slots_ref,
        info_ref,
        info_smem,
        held,
        sorted_,
        mirror,
        blocks,
        outgoing,
        tables,
        fixed,
        fixed_smem,
        table_smem,
        mirror_smem,
        strip,
        spectra,
        parts,
        cells,
        shifted,
        canvas,
        warped,
        send_sem,
        recv_sem,
        far_sem,
        slot_sem,
        local_sem,
        table_sem,
        out_sem,
    ) = rest
    gz, gy, gx = lax.axis_index("gz"), lax.axis_index("gy"), lax.axis_index("gx")
    half, core = gy // 2, gy % 2
    place = core * 4 + gx
    far_gy = 3 - gy
    near_gy = gy + 1 - 2 * core

    barrier = pltpu.get_barrier_semaphore()

    def greet(step, carry):
        pl.semaphore_signal(
            barrier, inc=1, device_id={"gz": lax.rem(gz + step, SECTIONS)}, device_id_type=MESH
        )
        return carry

    inner = (gy == 1) | (gy == 2)

    @pl.when(inner)
    def _():
        def greet_far(step, carry):
            section = lax.rem(gz + step, SECTIONS)
            pl.semaphore_signal(
                barrier, inc=1, device_id={"gz": section, "gy": far_gy}, device_id_type=MESH
            )
            return carry

        lax.fori_loop(1, SECTIONS, greet_far, 0)

    pl.semaphore_signal(barrier, inc=1, device_id={"gy": far_gy}, device_id_type=MESH)
    lax.fori_loop(1, SECTIONS, greet, 0)
    for step in range(1, 8):
        other_place = lax.rem(place + step, 8)
        pl.semaphore_signal(
            barrier,
            inc=1,
            device_id={"gy": 2 * half + other_place // 4, "gx": other_place % 4},
            device_id_type=MESH,
        )

    loads = [
        pltpu.make_async_copy(src, dst, table_sem.at[index])
        for index, (src, dst) in enumerate(zip(tables_hbm, tables_vmem))
    ]
    for load in loads:
        load.start()
    fixed[...] = jnp.round(flow_ref[...].astype(f32) * float(2**FIXED)).astype(jnp.int32)
    to_scalars = pltpu.make_async_copy(fixed, fixed_smem, local_sem)
    to_scalars.start()
    own_ref[pl.ds(HALO_ROWS, HEIGHT), pl.ds(LANES, WIDTH)] = tile_ref[...]
    top, bottom = pl.ds(0, HALO_ROWS), pl.ds(HALO_ROWS + HEIGHT, HALO_ROWS)
    left, right = pl.ds(0, LANES), pl.ds(LANES + WIDTH, LANES)
    middle = pl.ds(LANES, WIDTH)
    for ref in (own_ref, other_ref):

        @pl.when(gy == 0)
        def _():
            ref[top, middle] = jnp.zeros((HALO_ROWS, WIDTH), bf16)

        @pl.when(gy == 3)
        def _():
            ref[bottom, middle] = jnp.zeros((HALO_ROWS, WIDTH), bf16)

        @pl.when(gx == 0)
        def _():
            ref[:, left] = jnp.zeros((STRIP_ROWS, LANES), bf16)

        @pl.when(gx == 3)
        def _():
            ref[:, right] = jnp.zeros((STRIP_ROWS, LANES), bf16)

    lane = lax.broadcasted_iota(jnp.int32, (HEIGHT, LANES), 1)

    def cut_blocks(ref, base):
        for block in range(BLOCKS):
            start = STRIDE * block
            first = start // LANES * LANES
            shift = start - first
            width = LANES if shift + STRIDE <= LANES else 2 * LANES
            window = ref[:, first : first + width].astype(f32)
            if shift:
                window = pltpu.roll(window, width - shift, 1)[:, :LANES]
            blocks[base + block] = jnp.where(lane < STRIDE, window, 0.0).astype(bf16)

    def fill(kind, table):
        for target in range(8):
            base = 8 * (8 * half + target)
            for rank in range(2):
                block = table[0, base + 4 * rank]
                outgoing[kind, target, rank] = blocks[BLOCKS * kind + block]

    cut_blocks(tile_ref, 0)
    to_scalars.wait()
    fill_table(owner_ref, cell_ref, count_ref, fixed_smem, table_smem)
    to_vector = pltpu.make_async_copy(table_smem, tables.at[0], local_sem)
    to_vector.start()
    fill(0, table_smem)
    to_vector.wait()
    holds, mine = chunk_of(gz)
    @pl.when(inner)
    def _():
        pl.semaphore_wait(barrier, 2 * (SECTIONS - 1) + 8)

    @pl.when(jnp.logical_not(inner))
    def _():
        pl.semaphore_wait(barrier, SECTIONS - 1 + 8)

    line, upper = gz // 8, gz % 8 >= 4

    def far_section(step):
        to = jnp.where(upper, step // 4, 7 - step // 4)
        return 8 * lax.rem(line + 2 + step % 4, 4) + to

    def far_chunk(step):
        before = jnp.maximum(step - 1, 0)
        to = jnp.where(upper, before // 4, 5 - before // 4)
        return jnp.where(step == 0, CHUNKS - 1, 6 * lax.rem(line + 2 + before % 4, 4) + to)

    def scatter(step, carry):
        chunk = far_chunk(step)
        holder = holder_of(chunk)

        @pl.when(holder != gz)
        def _():
            pltpu.make_async_remote_copy(
                src_ref=chunk_at(tile_ref, chunk, 0, 0),
                dst_ref=held.at[gz],
                send_sem=send_sem.at[0],
                recv_sem=recv_sem.at[0],
                device_id={"gz": holder},
                device_id_type=MESH,
            ).start()

        return carry

    def copy(src, dst, slot, device):
        return pltpu.make_async_remote_copy(
            src_ref=src,
            dst_ref=dst,
            send_sem=far_sem.at[0, slot],
            recv_sem=far_sem.at[1, slot],
            device_id=device,
            device_id_type=MESH,
        )

    near = {"gy": near_gy}
    own_down = copy(
        tile_ref.at[pl.ds(HEIGHT - HALO_ROWS, HALO_ROWS), :], own_ref.at[top, middle], 0, near
    )
    own_up = copy(tile_ref.at[pl.ds(0, HALO_ROWS), :], own_ref.at[bottom, middle], 0, near)
    to_far = copy(tile_ref, mirror, 1, {"gy": far_gy})
    table_far = copy(tables.at[0], tables.at[1], 2, {"gy": far_gy})

    def send_slots(kind):
        def one(step, carry):
            target = lax.rem(place + step, 8)
            device = {"gy": 2 * half + target // 4, "gx": target % 4}
            for src, dst, row in (
                (outgoing.at[kind, target], slots_ref.at[kind, place], 0),
                (tables.at[kind], info_ref.at[kind, place], 1),
            ):
                pltpu.make_async_remote_copy(
                    src_ref=src,
                    dst_ref=dst,
                    send_sem=slot_sem.at[0, kind, row],
                    recv_sem=slot_sem.at[1, kind, row],
                    device_id=device,
                    device_id_type=MESH,
                ).start()
            return carry

        lax.fori_loop(1, 8, one, 0)
        slots_ref[kind, place] = outgoing[kind, place]
        info_ref[kind, place] = tables[kind]

    lax.fori_loop(0, CHUNKS, scatter, 0)
    table_far.start()
    to_far.start()

    @pl.when(core == 0)
    def _():
        own_down.start()

    @pl.when(core == 1)
    def _():
        own_up.start()

    send_slots(0)

    first_row = jnp.where(gy == 1, 2, 0)
    rim_chunk = mine - 5 * first_row
    holds_rim = holds & inner & (rim_chunk >= 0) & (rim_chunk < 15)
    rim_chunk = jnp.where(holds_rim, rim_chunk, 0)
    rim_row = jnp.where(gy == 1, 0, HALO_ROWS + HEIGHT)

    @pl.when(holds)
    def _():
        held[gz] = chunk_at(tile_ref, mine, 0, 0)[...]
        pltpu.make_async_copy(
            held.at[pl.ds(0, SECTIONS - 1)], held.at[pl.ds(0, SECTIONS - 1)], recv_sem.at[0]
        ).wait()
        for section in range(SECTIONS):
            sorted_[section] = held[partner_ref[0, section]]

        def deliver(step, carry):
            section = far_section(step)

            @pl.when(section != gz)
            def _():
                pltpu.make_async_remote_copy(
                    src_ref=sorted_.at[section],
                    dst_ref=chunk_at(other_ref, mine, HALO_ROWS, LANES),
                    send_sem=send_sem.at[1],
                    recv_sem=recv_sem.at[1],
                    device_id={"gz": section},
                    device_id_type=MESH,
                ).start()

            return carry

        def deliver_far(step, carry):
            section = lax.rem(gz + step, SECTIONS)
            pltpu.make_async_remote_copy(
                src_ref=sorted_.at[section],
                dst_ref=chunk_at(other_ref, rim_chunk, rim_row, LANES),
                send_sem=send_sem.at[2],
                recv_sem=recv_sem.at[2],
                device_id={"gz": section, "gy": far_gy},
                device_id_type=MESH,
            ).start()
            return carry

        def send_far():
            lax.fori_loop(0, SECTIONS, deliver_far, 0)

        pl.when(holds_rim)(send_far)
        lax.fori_loop(0, SECTIONS, deliver, 0)
        chunk_at(other_ref, mine, HALO_ROWS, LANES)[...] = sorted_[gz]


    def side_copies(ref, slot):
        to_right = copy(
            ref.at[:, pl.ds(WIDTH, LANES)], ref.at[:, left], slot, {"gx": jnp.minimum(gx + 1, 3)}
        )
        to_left = copy(
            ref.at[:, pl.ds(LANES, LANES)], ref.at[:, right], slot + 1, {"gx": jnp.maximum(gx - 1, 0)}
        )
        return to_right, to_left

    def start_sides(copies):
        @pl.when(gx < 3)
        def _():
            copies[0].start()

        @pl.when(gx > 0)
        def _():
            copies[1].start()

    def receive_sides(copies):
        @pl.when(gx > 0)
        def _():
            copies[0].wait_recv()

        @pl.when(gx < 3)
        def _():
            copies[1].wait_recv()

    def sent_sides(copies):
        @pl.when(gx < 3)
        def _():
            copies[0].wait_send()

        @pl.when(gx > 0)
        def _():
            copies[1].wait_send()

    chunks = held.at[pl.ds(0, CHUNKS)]
    fewer = held.at[pl.ds(0, CHUNKS - 1)]
    near_from = pl.ds(pl.multiple_of(HEIGHT - (HEIGHT - HALO_ROWS) * core, 16), HALO_ROWS)
    near_to = pl.ds(pl.multiple_of((HALO_ROWS + HEIGHT) * core, 16), HALO_ROWS)
    rest_rows = pl.ds(pl.multiple_of(HALO_ROWS * core, 16), HALO_ROWS + HEIGHT)
    from_right, from_left = pl.ds(WIDTH, LANES), pl.ds(LANES, LANES)
    after, before = jnp.minimum(gx + 1, 3), jnp.maximum(gx - 1, 0)
    other_near = copy(
        other_ref.at[near_from, middle], other_ref.at[near_to, middle], 5, {"gy": near_gy}
    )
    other_right = [
        copy(other_ref.at[rest_rows, from_right], other_ref.at[rest_rows, left], 6, {"gx": after}),
        copy(
            other_ref.at[near_from, from_right],
            other_ref.at[near_to, left],
            7,
            {"gy": near_gy, "gx": after},
        ),
    ]
    other_left = [
        copy(other_ref.at[rest_rows, from_left], other_ref.at[rest_rows, right], 8, {"gx": before}),
        copy(
            other_ref.at[near_from, from_left],
            other_ref.at[near_to, right],
            9,
            {"gy": near_gy, "gx": before},
        ),
    ]
    own_sides = side_copies(own_ref, 3)

    def pass_rows():
        @pl.when(holds)
        def _():
            pltpu.make_async_copy(fewer, fewer, recv_sem.at[1]).wait()

        @pl.when(jnp.logical_not(holds))
        def _():
            pltpu.make_async_copy(chunks, chunks, recv_sem.at[1]).wait()

        @pl.when(inner)
        def _():
            rim = held.at[pl.ds(0, 15)]
            pltpu.make_async_copy(rim, rim, recv_sem.at[2]).wait()

        other_near.start()

        @pl.when(gx < 3)
        def _():
            for one in other_right:
                one.start()

        @pl.when(gx > 0)
        def _():
            for one in other_left:
                one.start()

    def receive_rims():
        other_near.wait_recv()

        @pl.when(gx > 0)
        def _():
            for one in other_right:
                one.wait_recv()

        @pl.when(gx < 3)
        def _():
            for one in other_left:
                one.wait_recv()

    def take_mirror():
        @pl.when(core == 1)
        def _():
            own_down.wait_recv()

        @pl.when(core == 0)
        def _():
            own_up.wait_recv()

        table_far.wait_recv()
        fetch = pltpu.make_async_copy(tables.at[1], mirror_smem, local_sem)
        fetch.start()
        to_far.wait_recv()

        @pl.when(gy == 1)
        def _():
            own_ref[bottom, middle] = mirror[pl.ds(0, HALO_ROWS), :]

        @pl.when(gy == 2)
        def _():
            own_ref[top, middle] = mirror[pl.ds(HEIGHT - HALO_ROWS, HALO_ROWS), :]

        start_sides(own_sides)
        cut_blocks(mirror, BLOCKS)
        fetch.wait()
        fill(1, mirror_smem)
        send_slots(1)

    stores = [
        pltpu.make_async_copy(parts, parts_hbm, out_sem.at[0]),
        pltpu.make_async_copy(warped, warped_hbm, out_sem.at[1]),
    ]

    def own_spectra():
        receive_sides(own_sides)
        for load in loads:
            load.wait()
        scales = forward(own_ref, strip, spectra, parts, *tables_vmem)
        stores[0].start()
        for patch, scale in enumerate(scales):
            scale_ref[patch : patch + 1, :] = jnp.broadcast_to(scale, (1, LANES))

    def warp():
        for kind in range(2):
            seven, seven_info = slots_ref.at[kind, pl.ds(0, 7)], info_ref.at[kind, pl.ds(0, 7)]
            pltpu.make_async_copy(seven, seven, slot_sem.at[1, kind, 0]).wait()
            pltpu.make_async_copy(seven_info, seven_info, slot_sem.at[1, kind, 1]).wait()
        fetch = pltpu.make_async_copy(info_ref, info_smem, local_sem)
        fetch.start()
        cells[...] = jnp.zeros_like(cells)
        shifted[...] = jnp.zeros_like(shifted)
        fetch.wait()
        add_up(slots_ref, info_smem, 8 * (4 * gy + gx), cells, shifted, canvas, warped)
        stores[1].start()

    take_mirror()
    own_spectra()
    pass_rows()
    warp()
    receive_rims()

    for kind in range(2):
        seven, seven_info = slots_ref.at[kind, pl.ds(0, 7)], info_ref.at[kind, pl.ds(0, 7)]
        pltpu.make_async_copy(seven, seven, slot_sem.at[0, kind, 0]).wait()
        pltpu.make_async_copy(seven_info, seven_info, slot_sem.at[0, kind, 1]).wait()

    @pl.when(holds)
    def _():
        pltpu.make_async_copy(fewer, fewer, send_sem.at[0]).wait()
        all_but_one = held.at[pl.ds(0, SECTIONS - 1)]
        pltpu.make_async_copy(all_but_one, all_but_one, send_sem.at[1]).wait()

    @pl.when(jnp.logical_not(holds))
    def _():
        pltpu.make_async_copy(chunks, chunks, send_sem.at[0]).wait()

    @pl.when(core == 0)
    def _():
        own_down.wait_send()

    @pl.when(core == 1)
    def _():
        own_up.wait_send()

    to_far.wait_send()
    table_far.wait_send()

    other_near.wait_send()

    @pl.when(gx < 3)
    def _():
        for one in other_right:
            one.wait_send()

    @pl.when(gx > 0)
    def _():
        for one in other_left:
            one.wait_send()

    @pl.when(holds_rim)
    def _():
        every = held.at[pl.ds(0, SECTIONS)]
        pltpu.make_async_copy(every, every, send_sem.at[2]).wait()

    sent_sides(own_sides)
    for store in stores:
        store.wait()


def split(value):
    high = value.astype(bf16)
    return high, (value - high.astype(f32)).astype(bf16)


def dot(left, right):
    return jnp.dot(left, right, preferred_element_type=f32)


def forward(ref, strip, spectra, parts, rows_both, row_sums, columns_twice, columns_low):
    lane = lax.broadcasted_iota(jnp.int32, (PATCH_SIZE, LANES), 1)
    means, squares = [], []
    for block in range(HALVES):
        start = LANES - 40 + STRIDE * block
        first = start // LANES * LANES
        shift = start - first
        width = LANES if shift + STRIDE <= LANES else 2 * LANES
        window = ref[8 : 8 + PATCH_SIZE, first : first + width].astype(f32)
        window = pltpu.roll(window, width - shift, 1)[:, :LANES]
        window = jnp.where(lane < STRIDE, window, 0.0)
        mean = jnp.sum(window, keepdims=True) * (1.0 / (PATCH_SIZE * STRIDE))
        centred = jnp.where(lane < STRIDE, window - mean, 0.0)
        means.append(mean)
        squares.append(jnp.sum(centred * centred, keepdims=True))
        strip[:, pl.ds(block * LANES, LANES)] = window.astype(bf16)

    level = sum(means) * (1.0 / HALVES) * row_sums[...]
    for block in range(HALVES):
        both = dot(rows_both[...], strip[:, pl.ds(block * LANES, LANES)])
        value = both[: 2 * WAVES] + both[2 * WAVES :] - level
        high, low = split(value)
        spectra[block, :, :LANES] = high
        spectra[block, :, LANES:] = low
    for block in range(HALVES):
        parts[block] = dot(spectra[block], columns_twice[...]) + dot(
            spectra[block, :, :LANES], columns_low[...]
        )

    count = PATCH_SIZE * STRIDE
    scales = []
    for patch in range(PATCH_COLS):
        gap = means[patch] - means[patch + 1]
        spread = (squares[patch] + squares[patch + 1] + gap * gap * (count / 2)) * (0.5 / count)
        scales.append(1.0 / jnp.sqrt(spread + epsilon))
    return scales


def add_up(slots_ref, info_smem, mine, cells, shifted, canvas, warped):
    unit = 1.0 / 2**FIXED

    def entries(source, carry):
        values, named = [], []
        for kind in range(2):
            for rank in range(2):
                base = mine + 4 * rank
                named.append(info_smem[kind, source, 0, base + 1])
                down = info_smem[kind, source, 0, base + 2]
                across = info_smem[kind, source, 0, base + 3]
                whole_down = jnp.clip(down >> FIXED, 1 - MARGIN, MARGIN - 1)
                whole_across = jnp.clip(across >> FIXED, 1 - MARGIN, MARGIN - 1)
                part_down = (down & (2**FIXED - 1)).astype(f32) * unit
                part_across = (across & (2**FIXED - 1)).astype(f32) * unit
                block = slots_ref[kind, source, rank].astype(f32)
                here = pltpu.roll(block, whole_across + MARGIN, 1)
                after = pltpu.roll(here, 1, 1)
                room = shifted.at[2 * kind + rank]
                room[pl.ds(MARGIN, HEIGHT), :] = here * (1.0 - part_across) + after * part_across
                here = room[pl.ds(MARGIN - whole_down, HEIGHT), :]
                after = room[pl.ds(MARGIN - 1 - whole_down, HEIGHT), :]
                value = here * (1.0 - part_down) + after * part_down
                values.append(value.astype(bf16).astype(f32))
        for cell in range(BLOCKS):
            total = cells[cell]
            for value, name in zip(values, named):
                total = total + value * (name == cell).astype(f32)
            cells[cell] = total
        return carry

    lax.fori_loop(0, 8, entries, 0)
    canvas[...] = jnp.zeros_like(canvas)
    for cell in range(BLOCKS):
        start = LANES - MARGIN + STRIDE * cell
        first = start // LANES * LANES
        shift = start - first
        wide = jnp.concatenate([cells[cell], jnp.zeros((HEIGHT, LANES), f32)], axis=1)
        if shift:
            wide = pltpu.roll(wide, shift, 1)
        canvas[:, first : first + 2 * LANES] = canvas[:, first : first + 2 * LANES] + wide
    warped[...] = canvas[:, LANES : LANES + WIDTH]


def compute_kernel(other_ref, parts_hbm, warped_in, scale_ref, mask_ref, *rest):
    tables_hbm, (correlation_hbm, warped_hbm), rest = rest[:7], rest[7:9], rest[9:]
    tables_vmem, rest = rest[:7], rest[7:]
    strip, spectra, own_parts, parts, result, table_sem, part_sem, out_sem = rest
    loads = [
        pltpu.make_async_copy(src, dst, table_sem.at[index])
        for index, (src, dst) in enumerate(zip(tables_hbm, tables_vmem))
    ]
    for load in loads:
        load.start()
    own_load = pltpu.make_async_copy(parts_hbm, own_parts, part_sem)
    own_load.start()
    stores = [pltpu.make_async_copy(warped_in, warped_hbm, out_sem.at[PATCH_COLS])]
    stores[0].start()
    back_columns_high, back_columns_low, back_rows = tables_vmem[4:]
    for load in loads[:4]:
        load.wait()
    scales = forward(other_ref, strip, spectra, parts, *tables_vmem[:4])
    for load in [*loads[4:], own_load]:
        load.wait()

    row = lax.broadcasted_iota(jnp.int32, (WAVES, LANES), 0)
    column = lax.broadcasted_iota(jnp.int32, (WAVES, LANES), 1)
    constant = (row == 0) & (column == 0)
    odd = column % 2 == 1

    def spectrum(ref, first):
        def one(rows, lanes):
            later = ref[first + 1, rows, lanes]
            return ref[first, rows, lanes] + jnp.where(odd, -later, later)

        upper, lower = pl.ds(0, WAVES), pl.ds(WAVES, WAVES)
        low, high = pl.ds(0, LANES), pl.ds(LANES, LANES)
        a = jnp.where(constant, 0.0, one(upper, low))
        return a, one(lower, high), one(lower, low), one(upper, high)

    for patch in range(PATCH_COLS):
        scale = mask_ref[0, patch].astype(f32) * (2.0 / PATCH_SIZE**3)
        scale = scale * scales[patch] * scale_ref[patch : patch + 1, :]
        a, b, c, d = spectrum(own_parts, patch)
        e, f, g, h = spectrum(parts, patch)
        even_real = (a * e + b * f + c * g + d * h) * scale
        odd_real = (c * h + d * g - a * f - b * e) * scale
        even_imag = (c * e - d * f - a * g + b * h) * scale
        odd_imag = (d * e - c * f - a * h + b * g) * scale
        joined = jnp.concatenate(
            [
                jnp.concatenate([even_real, -odd_imag], axis=1),
                jnp.concatenate([even_imag, odd_real], axis=1),
            ],
            axis=0,
        )
        high, low = split(joined)
        both = dot(jnp.concatenate([high, low], axis=0), back_columns_high[...])
        half = both[: 2 * WAVES] + both[2 * WAVES :] + dot(high, back_columns_low[...])
        high, low = split(half)
        both = dot(back_rows[...], high)
        result[patch] = (
            both[:PATCH_SIZE] + both[PATCH_SIZE:] + dot(back_rows[:PATCH_SIZE, :], low)
        )
        stores.append(
            pltpu.make_async_copy(result.at[patch], correlation_hbm.at[patch], out_sem.at[patch])
        )
        stores[-1].start()
    for store in stores:
        store.wait()


VMEM = pl.BlockSpec(memory_space=pltpu.VMEM)
SMEM = pl.BlockSpec(memory_space=pltpu.SMEM)
ANY = pl.BlockSpec(memory_space=pl.ANY)


def body(tables, images, partner, patch_mask, flows, dest_count, dest_owner, dest_cell):
    space = [pltpu.VMEM(table.shape, table.dtype) for table in tables]
    parts_shape = (HALVES, 2 * WAVES, 2 * LANES)
    other, parts, warped, scale = pl.pallas_call(
        exchange_kernel,
        out_shape=[
            jax.ShapeDtypeStruct((STRIP_ROWS, STRIP_COLS), bf16),
            jax.ShapeDtypeStruct(parts_shape, f32),
            jax.ShapeDtypeStruct((HEIGHT, WIDTH), f32),
            jax.ShapeDtypeStruct((PATCH_COLS, LANES), f32),
        ],
        in_specs=[VMEM, SMEM, SMEM, SMEM, SMEM, VMEM] + [ANY] * 4,
        out_specs=[VMEM, ANY, ANY, VMEM],
        scratch_shapes=space[:4]
        + [
            pltpu.VMEM((STRIP_ROWS, STRIP_COLS), bf16),
            pltpu.VMEM((2, 8, 2, HEIGHT, LANES), bf16),
            pltpu.VMEM((2, 8, 1, 128), jnp.int32),
            pltpu.SMEM((2, 8, 1, 128), jnp.int32),
            pltpu.VMEM((SECTIONS, 16, LANES), bf16),
            pltpu.VMEM((SECTIONS, 16, LANES), bf16),
            pltpu.VMEM((HEIGHT, WIDTH), bf16),
            pltpu.VMEM((2 * BLOCKS, HEIGHT, LANES), bf16),
            pltpu.VMEM((2, 8, 2, HEIGHT, LANES), bf16),
            pltpu.VMEM((2, 1, 128), jnp.int32),
            pltpu.VMEM((2, BLOCKS), jnp.int32),
            pltpu.SMEM((2, BLOCKS), jnp.int32),
            pltpu.SMEM((1, 128), jnp.int32),
            pltpu.SMEM((1, 128), jnp.int32),
            pltpu.VMEM((PATCH_SIZE, HALVES * LANES), bf16),
            pltpu.VMEM(parts_shape, bf16),
            pltpu.VMEM(parts_shape, f32),
            pltpu.VMEM((BLOCKS, HEIGHT, LANES), f32),
            pltpu.VMEM((4, 128, LANES), f32),
            pltpu.VMEM((HEIGHT, STRIP_COLS), f32),
            pltpu.VMEM((HEIGHT, WIDTH), f32),
            pltpu.SemaphoreType.DMA((3,)),
            pltpu.SemaphoreType.DMA((3,)),
            pltpu.SemaphoreType.DMA((2, 10)),
            pltpu.SemaphoreType.DMA((2, 2, 2)),
            pltpu.SemaphoreType.DMA,
            pltpu.SemaphoreType.DMA((4,)),
            pltpu.SemaphoreType.DMA((2,)),
        ],
        compiler_params=pltpu.CompilerParams(
            collective_id=0, has_side_effects=True, vmem_limit_bytes=VMEM_BYTES
        ),
    )(
        images[0],
        partner[0],
        dest_owner[0, 0, 0].T,
        dest_cell[0, 0, 0].T,
        dest_count[0, 0],
        flows[0, 0, 0].T,
        *tables[:4],
    )
    correlation, warped = pl.pallas_call(
        compute_kernel,
        out_shape=[
            jax.ShapeDtypeStruct((PATCH_COLS, PATCH_SIZE, PATCH_SIZE), f32),
            jax.ShapeDtypeStruct((HEIGHT, WIDTH), f32),
        ],
        in_specs=[VMEM, ANY, ANY, VMEM, SMEM] + [ANY] * 7,
        out_specs=[ANY, ANY],
        scratch_shapes=space
        + [
            pltpu.VMEM((PATCH_SIZE, HALVES * LANES), bf16),
            pltpu.VMEM(parts_shape, bf16),
            pltpu.VMEM(parts_shape, f32),
            pltpu.VMEM(parts_shape, f32),
            pltpu.VMEM((PATCH_COLS, PATCH_SIZE, PATCH_SIZE), f32),
            pltpu.SemaphoreType.DMA((7,)),
            pltpu.SemaphoreType.DMA,
            pltpu.SemaphoreType.DMA((PATCH_COLS + 1,)),
        ],
        compiler_params=pltpu.CompilerParams(vmem_limit_bytes=VMEM_BYTES),
    )(other, parts, warped, scale, patch_mask[0], *tables)
    return correlation[None, None], warped[None]


def solution(mesh):
    placed = (
        P("gz", "gy", "gx"),
        P("gy", "gx", None),
        P("gz", "gy", "gx"),
        P("gz", "gy", "gx", None, None),
        P("gz", "gy", "gx", None),
        P("gz", "gy", "gx", None, None),
        P("gz", "gy", "gx", None, None),
    )
    tables = tuple(jnp.asarray(table) for table in make_tables())
    return jax.shard_map(
        functools.partial(body, tables),
        mesh=mesh,
        in_specs=placed,
        out_specs=(P("gz", "gy", "gx", None, None), P("gz", "gy", "gx")),
        check_vma=False,
    )
```
